32 devices in a mesh: groups: 2 (over y), space: 4 (over z), tm: 2 (over x), chan: 2 (over core).
Axes of the slice: x: 2, y: 2, z: 4, core: 2. Of those that a mesh axis runs over, the one named last changes fastest.
Arguments:
- hidden_states: bfloat16 [8, 4, 64, 512], P(('groups', 'tm'), 'space', None, 'chan'), parts along dimension 0, may hold values from -25 to 25
- first_gain: float32 [512], P('chan'), may hold values from 0.1 to 1.9
- second_gain: float32 [512], P('chan'), may hold values from 0.1 to 1.9
- query_weight: bfloat16 [512, 512], replicated, may hold values from -0.4861359 to 0.4861359
- key_weight: bfloat16 [512, 512], replicated, may hold values from -0.4861359 to 0.4861359
- value_weight: bfloat16 [512, 512], replicated, may hold values from -0.25 to 0.25
- out_weight: bfloat16 [512, 512], replicated, may hold values from -0.25 to 0.25
- conv_kernel: bfloat16 [3, 3, 3, 512, 512], P(None, None, None, 'tm', 'chan'), may hold values from -0.0546875 to 0.0546875
Outputs:
- attended: bfloat16 [8, 4, 64, 512], P(('groups', 'tm'), 'space', None, 'chan'), parts along dimension 0
- convolved: bfloat16 [8, 4, 64, 512], P(('groups', 'tm'), 'space', None, 'chan'), parts along dimension 0
The draws below stay inside these ranges and needn't reach their ends.
There are 2 independent parts, one for each index of `groups`. The reference program is written for one: setup_inputs(seed, part) draws one part's arguments, and reference() takes and returns one part's arrays. A program takes and returns all parts, laid end to end along the dimension named above; an argument that names none is the same for every part. Nothing has to cross between parts.
All inputs are finite; a program needn't handle non-finite values.
Results may differ from the reference program's by a relative error of at most 0.012.
The reference program's roundings to bfloat16 on the way count: a program that leaves them out, or rounds other values in their place, can miss the bound.
Values may be sent and summed in bfloat16 or wider, within the bound.
No kernel may reach another device: no remote copies, remote signals or barrier semaphores. Data moves between devices by JAX's collectives and lax.ppermute only.
A program may use at most 64 MiB of HBM per device.

```python
import jax
import jax.numpy as jnp
from jax import lax

D = 512
NGROUP = 32
W = 64
NF = 4
NH = 4


def draw_hidden_states(key, part):
    normal_key = jax.random.fold_in(key, 1)
    channel_key = jax.random.fold_in(key, 2)
    jitter_key = jax.random.fold_in(key, 3)
    frame_pos = jnp.arange(NF, dtype=jnp.float32) / (NF - 1)
    row_pos = jnp.arange(NH, dtype=jnp.float32) / (NH - 1)
    exponent = 0.5 * frame_pos[:, None] + 0.5 * row_pos[None, :] - 1.0
    jitter = jax.random.uniform(jitter_key, (NF, NH, W), minval=-0.1, maxval=0.1)
    token_scale = 10.0 ** (exponent[:, :, None] + jitter)
    channel_scale = jnp.exp(jax.random.uniform(channel_key, (D,), minval=jnp.log(0.5), maxval=jnp.log(5.0)))
    base = jnp.clip(jax.random.normal(normal_key, (NF, NH, W, D)), -3.5, 3.5)
    return (base * token_scale[:, :, :, None] * channel_scale).astype(jnp.bfloat16)


def drawn_pair(key):
    first = jnp.clip(jax.random.normal(jax.random.fold_in(key, 12), (D, D)), -4.5, 4.5)
    second = jnp.clip(jax.random.normal(jax.random.fold_in(key, 13), (D, D)), -4.5, 4.5)
    return (first, second)


def draw_query_weight(key, part):
    first, second = drawn_pair(key)
    result = first
    return (result * D ** (-0.5)).astype(jnp.bfloat16)


def draw_key_weight(key, part):
    first, second = drawn_pair(key)
    result = second
    return (result * D ** (-0.5)).astype(jnp.bfloat16)


def block_scale(own_key, extent, split, smallest, largest):
    def one(dim, parts):
        draws = jax.random.uniform(jax.random.fold_in(jax.random.fold_in(own_key, 6), dim), (parts,), jnp.float32, smallest / len(split), largest / len(split))
        return jnp.repeat(jnp.exp(draws), extent[dim] // parts).reshape((-1,) + (1,) * (len(extent) - dim - 1))

    loudness = one(*split[0])
    for cut in split[1:]:
        loudness = loudness * one(*cut)
    return loudness


def gaussian(rng, extent, scale, limit, split=(), held_as=jnp.bfloat16):
    gain = block_scale(rng, extent, split, -0.22, 0.18) if split else 1.0
    drawn = jax.random.normal(rng, extent, jnp.float32) * scale * gain
    return jnp.minimum(jnp.maximum(drawn, -limit), limit).astype(held_as)


def setup_inputs(seed: int = 0, part: int = 0) -> dict:
    arg_keys = jax.random.split(jax.random.key(seed), 9)
    own_keys = jax.random.split(jax.random.fold_in(arg_keys[8], part), 9)
    return {
        "hidden_states": draw_hidden_states(jax.random.fold_in(jax.random.fold_in(arg_keys[8], part), 71), part),
        "first_gain": jnp.clip(1.0 + 0.18 * jax.random.normal(arg_keys[1], (D,), jnp.float32), 0.1, 1.9),
        "second_gain": jnp.clip(1.0 + 0.18 * jax.random.normal(arg_keys[2], (D,), jnp.float32), 0.1, 1.9),
        "query_weight": draw_query_weight(jax.random.fold_in(arg_keys[8], 71), part),
        "key_weight": draw_key_weight(jax.random.fold_in(arg_keys[8], 71), part),
        "value_weight": gaussian(arg_keys[5], (D, D), D ** -0.5, 0.25),
        "out_weight": gaussian(arg_keys[6], (D, D), D ** -0.5, 0.25),
        "conv_kernel": gaussian(arg_keys[7], (3, 3, 3, D, D), (27 * D) ** -0.5, 0.0546875, ((3, 2), (4, 2))),
    }


EPSILON = 1e-06

def group_norm(source, gain_vector):
    grouped = source.reshape(-1, NGROUP, D // NGROUP)
    centre = lax.optimization_barrier(jnp.mean(grouped, axis=(0, 2)))
    shifted = grouped - centre[None, :, None]
    spread = lax.optimization_barrier(jnp.mean(shifted * shifted, axis=(0, 2)))
    scaled = shifted * lax.rsqrt(spread + EPSILON)[None, :, None]
    return scaled.reshape(source.shape) * gain_vector

def reference(hidden_states, first_gain, second_gain, query_weight, key_weight, value_weight, out_weight, conv_kernel):
    source = hidden_states.astype(jnp.float32)
    normed = group_norm(source, first_gain).astype(jnp.bfloat16)
    frame_tokens = normed.reshape(NF, NH * W, D)

    def frame_attention(tokens):
        queries = jnp.dot(tokens, query_weight, preferred_element_type=jnp.float32).astype(jnp.bfloat16)
        keyed = jnp.dot(tokens, key_weight, preferred_element_type=jnp.float32).astype(jnp.bfloat16)
        valued = jnp.dot(tokens, value_weight, preferred_element_type=jnp.float32).astype(jnp.bfloat16)
        scores = jnp.dot(queries, keyed.T, preferred_element_type=jnp.float32) * D ** (-0.5)
        peaked = lax.optimization_barrier(jnp.max(scores, axis=1))
        weights = jnp.exp(scores - peaked[:, None])
        mass = lax.optimization_barrier(jnp.sum(weights, axis=1))
        mixed = jnp.dot(weights.astype(jnp.bfloat16), valued, preferred_element_type=jnp.float32)
        mixed = (mixed / mass[:, None]).astype(jnp.bfloat16)
        return jnp.dot(mixed, out_weight, preferred_element_type=jnp.float32).astype(jnp.bfloat16)
    attended = lax.map(frame_attention, frame_tokens).reshape(source.shape)
    resid = source + attended.astype(jnp.float32)
    activated = jax.nn.silu(group_norm(resid, second_gain)).astype(jnp.bfloat16)
    convolved = lax.conv_general_dilated(activated.astype(jnp.float32)[None], conv_kernel.astype(jnp.float32), (1, 1, 1), [(2, 0), (1, 1), (1, 1)], dimension_numbers=('NDHWC', 'DHWIO', 'NDHWC'), precision=lax.Precision.HIGHEST)[0]
    return (attended, convolved.astype(jnp.bfloat16))
```

```python
import functools

import jax
import jax.numpy as jnp
from jax import lax
from jax.experimental import pallas as pl
from jax.experimental.pallas import tpu as pltpu
from jax.sharding import PartitionSpec as P

D = 512
NGROUP = 32


EPSILON = 1e-06


def shifted_2(x, axis, by):
    peers = lax.axis_size(axis)
    pairs = [(i, i + by) for i in range(peers) if 0 <= i + by < peers]
    return lax.ppermute(x, axis, pairs)


def padded_2(cells, sides, width):
    for axis, dim in sides:
        count = lax.axis_size(axis)
        ends = count - 1
        head = lax.slice_in_dim(cells, 0, width, axis=dim)
        tail = lax.slice_in_dim(cells, cells.shape[dim] - width, cells.shape[dim], axis=dim)
        cells = jnp.concatenate(
            [
                lax.ppermute(tail, axis, [(i, (i + 1) % count) for i in range(ends)]),
                cells,
                lax.ppermute(head, axis, [((i + 1) % count, i) for i in range(ends)]),
            ],
            axis=dim,
        )
    return cells


def normalize(source, gain_vector):
    channels = source.shape[3]
    group_width = D // NGROUP
    grouped = source.reshape(-1, channels // group_width, group_width)
    population = grouped.shape[0] * group_width * lax.axis_size("space") * lax.axis_size("tm")
    group_sums, group_squares = lax.psum(
        (jnp.sum(grouped, axis=(0, 2)), jnp.sum(grouped * grouped, axis=(0, 2))), ("space", "tm")
    )
    centre = group_sums / population
    spread = jnp.maximum(group_squares / population - centre * centre, 0.0)
    shifted = grouped - centre[None, :, None]
    scaled = shifted * lax.rsqrt(spread + EPSILON)[None, :, None]
    return scaled.reshape(source.shape) * gain_vector


def attend(normed, query_weight, key_weight, value_weight, out_weight):
    frame_count, row_count, col_count, channels = normed.shape
    token_count = frame_count * row_count * col_count
    tokens = normed.reshape(token_count, channels)
    halves = lax.all_to_all(tokens, "chan", split_axis=0, concat_axis=1, tiled=True)
    half_rows = halves.shape[0]
    queries = jnp.dot(halves, query_weight, preferred_element_type=jnp.float32).astype(jnp.bfloat16)
    keyed = jnp.dot(halves, key_weight, preferred_element_type=jnp.float32).astype(jnp.bfloat16)
    valued = jnp.dot(halves, value_weight, preferred_element_type=jnp.float32).astype(jnp.bfloat16)
    score_scale = D ** (-0.5)
    running_max = jnp.full((half_rows,), -1e30, jnp.float32)
    key_piece = lax.all_gather(keyed, "space", axis=0, tiled=True)
    value_piece = lax.all_gather(valued, "space", axis=0, tiled=True)
    scores = jnp.dot(queries, key_piece.T, preferred_element_type=jnp.float32) * score_scale
    newest_max = jnp.maximum(running_max, jnp.max(scores, axis=1))
    weights = jnp.exp(scores - newest_max[:, None])
    running_sum = jnp.sum(weights, axis=1)
    accumulated = jnp.dot(
        weights.astype(jnp.bfloat16), value_piece, preferred_element_type=jnp.float32
    )
    mixed = (accumulated / running_sum[:, None]).astype(jnp.bfloat16)
    projected = jnp.dot(mixed, out_weight, preferred_element_type=jnp.float32).astype(jnp.bfloat16)
    returned = lax.all_to_all(projected, "chan", split_axis=1, concat_axis=0, tiled=True)
    return returned.reshape(frame_count, row_count, col_count, channels)


def join_channels(activated):
    return lax.all_gather(activated, "chan", axis=3, tiled=True)


def extend(frames_in):
    earlier = shifted_2(frames_in, "tm", 1)
    timed = jnp.concatenate([earlier, frames_in], axis=0)
    rimmed = padded_2(timed, (("space", 1),), 1)
    return jnp.pad(rimmed, ((0, 0), (0, 0), (1, 1), (0, 0)))


def convolve(activated, conv_kernel):
    frame_count, row_count, col_count = (activated.shape[0], activated.shape[1], activated.shape[2])
    padded = extend(join_channels(activated))
    out_width = conv_kernel.shape[4]
    initial = jnp.zeros((frame_count * row_count * col_count, out_width), jnp.float32)
    running_total = initial
    piece = lax.all_gather(conv_kernel, "tm", axis=3, tiled=True)
    for time_tap in range(3):
        for row_tap in range(3):
            for col_tap in range(3):
                window = padded[
                    time_tap : time_tap + frame_count,
                    row_tap : row_tap + row_count,
                    col_tap : col_tap + col_count,
                ]
                window = window.reshape(frame_count * row_count * col_count, piece.shape[3])
                running_total = running_total + jnp.dot(
                    window, piece[time_tap, row_tap, col_tap], preferred_element_type=jnp.float32
                )
    return running_total.reshape(frame_count, row_count, col_count, out_width).astype(jnp.bfloat16)


def split_plan(
    hidden_states,
    first_gain,
    second_gain,
    query_weight,
    key_weight,
    value_weight,
    out_weight,
    conv_kernel,
):
    source = hidden_states.astype(jnp.float32)
    normed = normalize(source, first_gain).astype(jnp.bfloat16)
    attended = attend(normed, query_weight, key_weight, value_weight, out_weight)
    resid = source + attended.astype(jnp.float32)
    activated = jax.nn.silu(normalize(resid, second_gain)).astype(jnp.bfloat16)
    convolved = convolve(activated, conv_kernel)
    return (attended, convolved)


def exchange(x, axes, step):
    peers = lax.axis_size(axes)
    return lax.ppermute(x, axes, [(i, i ^ step) for i in range(peers)])


def pack_kernel(*refs):
    piece_refs, out_ref = refs[:-1], refs[-1]
    frames, cols, channels = piece_refs[0].shape
    blocks = out_ref.shape[0] // frames
    rows = len(piece_refs) // blocks
    for block in range(blocks):
        for row in range(rows):
            for frame in range(frames):
                out_ref[block * frames + frame, row] = piece_refs[row * blocks + block][frame]


def group_means(sums, count):
    channels = sums.shape[1]
    width = D // NGROUP
    left = lax.broadcasted_iota(jnp.int32, (channels, channels), 0) // width
    right = lax.broadcasted_iota(jnp.int32, (channels, channels), 1) // width
    member = (left == right).astype(jnp.float32)
    return jnp.dot(sums, member, precision=lax.Precision.HIGHEST, preferred_element_type=jnp.float32) / count


def moments(values, count):
    tokens, channels = values.shape
    parts = values.reshape(tokens // 8, 8, channels)
    sums = jnp.sum(jnp.sum(parts, axis=0), axis=0, keepdims=True)
    squares = jnp.sum(jnp.sum(parts * parts, axis=0), axis=0, keepdims=True)
    stacked = jnp.concatenate([sums, squares, jnp.zeros((6, channels), jnp.float32)], axis=0)
    means = group_means(stacked, count)
    centre = means[0:1]
    spread = jnp.maximum(means[1:2] - centre * centre, 0.0)
    return centre, lax.rsqrt(spread + EPSILON)


def main_kernel(
    mine_ref, other_ref, gains_ref, other_gains_ref, query_ref, key_ref, value_ref, out_weight_ref, kernel_ref,
    attended_ref, keep_ref, send_ref,
    normed, queries, keyed, valued, resid, activated,
):
    frames, rows, cols, channels = mine_ref.shape
    tokens = frames * rows * cols
    frame_tokens = rows * cols
    own_frames = attended_ref.shape[0]
    space = lax.axis_index("space")
    block = lax.axis_index("tm")
    half = lax.axis_index("chan")
    width = D // NGROUP
    count = tokens * width
    own_rows = pl.ds(pl.multiple_of(half * channels, channels), channels)
    other_rows = pl.ds(pl.multiple_of((1 - half) * channels, channels), channels)

    for side, (ref, gain_ref) in enumerate(((mine_ref, gains_ref), (other_ref, other_gains_ref))):
        values = ref[...].reshape(tokens, channels).astype(jnp.float32)
        centre, scale = moments(values, count)
        normed[side] = ((values - centre) * scale * gain_ref[0:1, :]).astype(jnp.bfloat16)

    for weight_ref, target in ((query_ref, queries), (key_ref, keyed), (value_ref, valued)):
        target[...] = (
            jnp.dot(normed[0], weight_ref[own_rows, :], preferred_element_type=jnp.float32)
            + jnp.dot(normed[1], weight_ref[other_rows, :], preferred_element_type=jnp.float32)
        ).astype(jnp.bfloat16)

    in_channels = kernel_ref.shape[3]
    in_cols = pl.ds(pl.multiple_of(block * in_channels, in_channels), in_channels)
    own_cols = pl.ds(pl.multiple_of(half * channels, channels), channels)
    mine_in = block == half
    for frame in range(frames):
        at = slice(frame * frame_tokens, (frame + 1) * frame_tokens)
        scores = lax.dot_general(
            queries[at, :], keyed[at, :], (((1,), (1,)), ((), ())), preferred_element_type=jnp.float32
        ) * (D ** (-0.5))
        weights = jnp.exp(scores - jnp.max(scores, axis=1, keepdims=True))
        mass = jnp.sum(weights, axis=1, keepdims=True)
        mixed = jnp.dot(weights.astype(jnp.bfloat16), valued[at, :], preferred_element_type=jnp.float32)
        mixed = (mixed / mass).astype(jnp.bfloat16)
        if frame < own_frames:
            attended_ref[frame, 0] = jnp.dot(
                mixed[:cols], out_weight_ref[:, own_cols], preferred_element_type=jnp.float32
            ).astype(jnp.bfloat16)
        projected = jnp.dot(
            mixed, out_weight_ref[:, in_cols], preferred_element_type=jnp.float32
        ).astype(jnp.bfloat16)
        source = jnp.where(mine_in, mine_ref[frame].astype(jnp.float32), other_ref[frame].astype(jnp.float32))
        resid[frame] = source + projected.astype(jnp.float32).reshape(rows, cols, in_channels)

    centre, scale = moments(resid[...].reshape(tokens, in_channels), count)
    gain = jnp.where(mine_in, gains_ref[1:2, :], other_gains_ref[1:2, :])
    for tap in range(3):
        row = space + (tap - 1)
        inside = jnp.logical_and(row >= 0, row < rows)
        place = jnp.where(inside, space ^ row, 0)
        for frame in range(frames):
            relative = ((frame // own_frames) ^ block) * own_frames + frame % own_frames
            values = (resid[relative, place] - centre) * scale * gain
            values = values / (1.0 + jnp.exp(-values))
            activated[tap, frame] = jnp.where(inside, values, 0.0).astype(jnp.bfloat16)

    out_channels = kernel_ref.shape[4]
    columns = [None] * 3
    for col_tap in range(3):
        total = None
        for time_tap in (2, 1, 0):
            late = 2 - time_tap
            shorter = None
            for row_tap in range(3):
                window = activated[row_tap, 0 : frames - late].reshape((frames - late) * cols, in_channels)
                term = jnp.dot(window, kernel_ref[time_tap, row_tap, col_tap], preferred_element_type=jnp.float32)
                shorter = term if shorter is None else shorter + term
            if late:
                shorter = jnp.concatenate([jnp.zeros((late * cols, out_channels), jnp.float32), shorter], axis=0)
            total = shorter if total is None else total + shorter
        columns[col_tap] = total
    place = lax.broadcasted_iota(jnp.int32, (frames * cols, out_channels), 0) % cols
    left = jnp.where(place == 0, 0.0, pltpu.roll(columns[0], 1, 0))
    right = jnp.where(place == cols - 1, 0.0, pltpu.roll(columns[2], frames * cols - 1, 0))
    summed = (columns[1] + left + right).reshape(frames, cols, out_channels)
    blocks = frames // own_frames
    for index in range(blocks):
        piece = summed[index * own_frames : (index + 1) * own_frames]

        @pl.when(index == block)
        def _():
            keep_ref[...] = piece

        @pl.when(index != block)
        def _():
            send_ref[(index ^ block) - 1] = piece.astype(jnp.bfloat16)


def gathered_plan(
    hidden_states, first_gain, second_gain, query_weight, key_weight, value_weight, out_weight, conv_kernel
):
    frames, _, cols, channels = hidden_states.shape
    rows, blocks = lax.axis_size("space"), lax.axis_size("tm")
    own = hidden_states.reshape(frames, cols, channels)
    gains = jnp.stack([first_gain, second_gain])
    other_gains = exchange(gains, "chan", 1)
    pieces = [own] + [exchange(own, ("space", "tm"), step) for step in range(1, rows * blocks)]
    mine = pl.pallas_call(
        pack_kernel,
        out_shape=jax.ShapeDtypeStruct((blocks * frames, rows, cols, channels), jnp.bfloat16),
        name="pack",
    )(*pieces)
    other = exchange(mine, "chan", 1)
    out_channels = conv_kernel.shape[4]
    in_channels = conv_kernel.shape[3]
    tokens = blocks * frames * rows * cols
    attended, keep, send = pl.pallas_call(
        main_kernel,
        out_shape=(
            jax.ShapeDtypeStruct((frames, 1, cols, channels), jnp.bfloat16),
            jax.ShapeDtypeStruct((frames, cols, out_channels), jnp.float32),
            jax.ShapeDtypeStruct((blocks - 1, frames, cols, out_channels), jnp.bfloat16),
        ),
        scratch_shapes=[
            pltpu.VMEM((2, tokens, channels), jnp.bfloat16),
            pltpu.VMEM((tokens, D), jnp.bfloat16),
            pltpu.VMEM((tokens, D), jnp.bfloat16),
            pltpu.VMEM((tokens, D), jnp.bfloat16),
            pltpu.VMEM((blocks * frames, rows, cols, in_channels), jnp.float32),
            pltpu.VMEM((3, blocks * frames, cols, in_channels), jnp.bfloat16),
        ],
        compiler_params=pltpu.CompilerParams(vmem_limit_bytes=40 * 1024 * 1024),
        name="block",
    )(mine, other, gains, other_gains, query_weight, key_weight, value_weight, out_weight, conv_kernel)
    total = keep
    for step in range(1, blocks):
        total = total + exchange(send[step - 1], "tm", step).astype(jnp.float32)
    return attended, total.astype(jnp.bfloat16).reshape(frames, 1, cols, out_channels)


def power_of_two(count):
    return count & (count - 1) == 0


def on_device(hidden_states, *others):
    frames, rows, cols, channels = hidden_states.shape
    spaces, blocks = lax.axis_size("space"), lax.axis_size("tm")
    tokens = frames * blocks * spaces * rows * cols
    fits = tokens * D <= 2 ** 20 and rows == 1 and lax.axis_size("chan") == 2 and blocks == 2
    if fits and power_of_two(spaces):
        return gathered_plan(hidden_states, *others)
    return split_plan(hidden_states, *others)


def solution(mesh):
    placed = (
        P(("groups", "tm"), "space", None, "chan"),
        P("chan"),
        P("chan"),
        P(),
        P(),
        P(),
        P(),
        P(None, None, None, "tm", "chan"),
    )
    return jax.shard_map(
        on_device,
        mesh=mesh,
        in_specs=placed,
        out_specs=(
            P(("groups", "tm"), "space", None, "chan"),
            P(("groups", "tm"), "space", None, "chan"),
        ),
        check_vma=False,
    )
```

```python
import functools

import jax
import jax.numpy as jnp
from jax import lax
from jax.experimental import pallas as pl
from jax.experimental.pallas import tpu as pltpu
from jax.sharding import PartitionSpec as P

D = 512
NGROUP = 32


EPSILON = 1e-06


def shifted_2(x, axis, by):
    peers = lax.axis_size(axis)
    pairs = [(i, i + by) for i in range(peers) if 0 <= i + by < peers]
    return lax.ppermute(x, axis, pairs)


def padded_2(cells, sides, width):
    for axis, dim in sides:
        count = lax.axis_size(axis)
        ends = count - 1
        head = lax.slice_in_dim(cells, 0, width, axis=dim)
        tail = lax.slice_in_dim(cells, cells.shape[dim] - width, cells.shape[dim], axis=dim)
        cells = jnp.concatenate(
            [
                lax.ppermute(tail, axis, [(i, (i + 1) % count) for i in range(ends)]),
                cells,
                lax.ppermute(head, axis, [((i + 1) % count, i) for i in range(ends)]),
            ],
            axis=dim,
        )
    return cells


def normalize(source, gain_vector):
    channels = source.shape[3]
    group_width = D // NGROUP
    grouped = source.reshape(-1, channels // group_width, group_width)
    population = grouped.shape[0] * group_width * lax.axis_size("space") * lax.axis_size("tm")
    group_sums, group_squares = lax.psum(
        (jnp.sum(grouped, axis=(0, 2)), jnp.sum(grouped * grouped, axis=(0, 2))), ("space", "tm")
    )
    centre = group_sums / population
    spread = jnp.maximum(group_squares / population - centre * centre, 0.0)
    shifted = grouped - centre[None, :, None]
    scaled = shifted * lax.rsqrt(spread + EPSILON)[None, :, None]
    return scaled.reshape(source.shape) * gain_vector


def attend(normed, query_weight, key_weight, value_weight, out_weight):
    frame_count, row_count, col_count, channels = normed.shape
    token_count = frame_count * row_count * col_count
    tokens = normed.reshape(token_count, channels)
    halves = lax.all_to_all(tokens, "chan", split_axis=0, concat_axis=1, tiled=True)
    half_rows = halves.shape[0]
    queries = jnp.dot(halves, query_weight, preferred_element_type=jnp.float32).astype(jnp.bfloat16)
    keyed = jnp.dot(halves, key_weight, preferred_element_type=jnp.float32).astype(jnp.bfloat16)
    valued = jnp.dot(halves, value_weight, preferred_element_type=jnp.float32).astype(jnp.bfloat16)
    score_scale = D ** (-0.5)
    running_max = jnp.full((half_rows,), -1e30, jnp.float32)
    key_piece = lax.all_gather(keyed, "space", axis=0, tiled=True)
    value_piece = lax.all_gather(valued, "space", axis=0, tiled=True)
    scores = jnp.dot(queries, key_piece.T, preferred_element_type=jnp.float32) * score_scale
    newest_max = jnp.maximum(running_max, jnp.max(scores, axis=1))
    weights = jnp.exp(scores - newest_max[:, None])
    running_sum = jnp.sum(weights, axis=1)
    accumulated = jnp.dot(
        weights.astype(jnp.bfloat16), value_piece, preferred_element_type=jnp.float32
    )
    mixed = (accumulated / running_sum[:, None]).astype(jnp.bfloat16)
    projected = jnp.dot(mixed, out_weight, preferred_element_type=jnp.float32).astype(jnp.bfloat16)
    returned = lax.all_to_all(projected, "chan", split_axis=1, concat_axis=0, tiled=True)
    return returned.reshape(frame_count, row_count, col_count, channels)


def join_channels(activated):
    return lax.all_gather(activated, "chan", axis=3, tiled=True)


def extend(frames_in):
    earlier = shifted_2(frames_in, "tm", 1)
    timed = jnp.concatenate([earlier, frames_in], axis=0)
    rimmed = padded_2(timed, (("space", 1),), 1)
    return jnp.pad(rimmed, ((0, 0), (0, 0), (1, 1), (0, 0)))


def convolve(activated, conv_kernel):
    frame_count, row_count, col_count = (activated.shape[0], activated.shape[1], activated.shape[2])
    padded = extend(join_channels(activated))
    out_width = conv_kernel.shape[4]
    initial = jnp.zeros((frame_count * row_count * col_count, out_width), jnp.float32)
    running_total = initial
    piece = lax.all_gather(conv_kernel, "tm", axis=3, tiled=True)
    for time_tap in range(3):
        for row_tap in range(3):
            for col_tap in range(3):
                window = padded[
                    time_tap : time_tap + frame_count,
                    row_tap : row_tap + row_count,
                    col_tap : col_tap + col_count,
                ]
                window = window.reshape(frame_count * row_count * col_count, piece.shape[3])
                running_total = running_total + jnp.dot(
                    window, piece[time_tap, row_tap, col_tap], preferred_element_type=jnp.float32
                )
    return running_total.reshape(frame_count, row_count, col_count, out_width).astype(jnp.bfloat16)


def split_plan(
    hidden_states,
    first_gain,
    second_gain,
    query_weight,
    key_weight,
    value_weight,
    out_weight,
    conv_kernel,
):
    source = hidden_states.astype(jnp.float32)
    normed = normalize(source, first_gain).astype(jnp.bfloat16)
    attended = attend(normed, query_weight, key_weight, value_weight, out_weight)
    resid = source + attended.astype(jnp.float32)
    activated = jax.nn.silu(normalize(resid, second_gain)).astype(jnp.bfloat16)
    convolved = convolve(activated, conv_kernel)
    return (attended, convolved)


GAIN_ROWS = 16


def exchange(x, axes, step):
    peers = lax.axis_size(axes)
    return lax.ppermute(x, axes, [(i, i ^ step) for i in range(peers)])


def stage_kernel(*refs):
    count = len(refs) // 2
    copies = [pltpu.make_async_copy(refs[i], refs[count + i], refs[-1].at[i]) for i in range(count)]
    for copy in copies:
        copy.start()
    for copy in copies:
        copy.wait()


def stage(arrays):
    size = sum(array.size * array.dtype.itemsize for array in arrays)
    return pl.pallas_call(
        stage_kernel,
        out_shape=tuple(jax.ShapeDtypeStruct(array.shape, array.dtype) for array in arrays),
        in_specs=[pl.BlockSpec(memory_space=pltpu.HBM)] * len(arrays),
        out_specs=tuple(pl.BlockSpec(memory_space=pltpu.VMEM) for _ in arrays),
        scratch_shapes=[pltpu.SemaphoreType.DMA((len(arrays),))],
        compiler_params=pltpu.CompilerParams(vmem_limit_bytes=1 << 20),
        cost_estimate=pl.CostEstimate(flops=0, bytes_accessed=2 * size, transcendentals=0),
        name="stage",
    )(*(in_hbm(array) for array in arrays))


def near_kernel(*refs):
    count = len(refs) - 8
    piece_refs, own_hbm, first_hbm, second_hbm, out_ref, own_ref, first_ref, second_ref, arrived = (
        refs[:count], *refs[count:]
    )
    copies = [
        pltpu.make_async_copy(own_hbm, own_ref, arrived.at[0]),
        pltpu.make_async_copy(first_hbm, first_ref, arrived.at[1]),
        pltpu.make_async_copy(second_hbm, second_ref, arrived.at[2]),
    ]
    for copy in copies:
        copy.start()
    size = own_ref.shape[0]
    for index, piece_ref in enumerate(piece_refs):
        out_ref[(index + 1) * size : (index + 2) * size, :] = piece_ref[...]
    for copy in copies:
        copy.wait()
    out_ref[:size, :] = own_ref[...]
    parts = []
    for gain_ref in (first_ref, second_ref):
        rest = gain_ref[...]
        for _ in range(3):
            rounded = rest.astype(jnp.bfloat16).astype(jnp.float32)
            parts.append(rounded)
            rest = rest - rounded
    parts.append(jnp.zeros((GAIN_ROWS - len(parts), out_ref.shape[1]), jnp.float32))
    end = out_ref.shape[0]
    out_ref[end - GAIN_ROWS : end, :] = jnp.concatenate(parts, axis=0).astype(jnp.bfloat16)


def pack_near(pieces, own, gains):
    size, channels = own.shape
    return pl.pallas_call(
        near_kernel,
        out_shape=jax.ShapeDtypeStruct(((len(pieces) + 1) * size + GAIN_ROWS, channels), own.dtype),
        in_specs=[pl.BlockSpec(memory_space=pltpu.VMEM)] * len(pieces) + [pl.BlockSpec(memory_space=pltpu.HBM)] * 3,
        scratch_shapes=[pltpu.VMEM(array.shape, array.dtype) for array in (own, *gains)]
        + [pltpu.SemaphoreType.DMA((3,))],
        compiler_params=pltpu.CompilerParams(vmem_limit_bytes=2 * 1024 * 1024),
        name="near",
    )(*pieces, *(in_hbm(array) for array in (own, *gains)))


def far_kernel(*refs):
    size = refs[0].shape[0]
    for index, piece_ref in enumerate(refs[:-1]):
        refs[-1][index * size : (index + 1) * size, :] = piece_ref[...]


def pack_far(pieces):
    size, channels = pieces[0].shape
    return pl.pallas_call(
        far_kernel,
        out_shape=jax.ShapeDtypeStruct((len(pieces) * size, channels), pieces[0].dtype),
        compiler_params=pltpu.CompilerParams(vmem_limit_bytes=2 * 1024 * 1024),
        name="far",
    )(*pieces)


def in_hbm(array):
    return pltpu.with_memory_space_constraint(array, pltpu.HBM)


def group_means(sums, count):
    channels = sums.shape[1]
    width = D // NGROUP
    left = lax.broadcasted_iota(jnp.int32, (channels, channels), 0) // width
    right = lax.broadcasted_iota(jnp.int32, (channels, channels), 1) // width
    member = (left == right).astype(jnp.float32)
    return jnp.dot(sums, member, precision=lax.Precision.HIGHEST, preferred_element_type=jnp.float32) / count


def moments(values, count):
    tokens, channels = values.shape
    parts = values.reshape(tokens // 8, 8, channels)
    sums = jnp.sum(jnp.sum(parts, axis=0), axis=0, keepdims=True)
    squares = jnp.sum(jnp.sum(parts * parts, axis=0), axis=0, keepdims=True)
    stacked = jnp.concatenate([sums, squares, jnp.zeros((6, channels), jnp.float32)], axis=0)
    means = group_means(stacked, count)
    centre = means[0:1]
    spread = jnp.maximum(means[1:2] - centre * centre, 0.0)
    return centre, lax.rsqrt(spread + EPSILON)


def main_kernel(
    near_ref, far_ref, other_near_ref, other_far_ref, query_ref, key_ref, value_ref, out_weight_ref, kernel_hbm,
    attended_ref, keep_ref, send_ref,
    normed, queries, keyed, valued, resid, activated, kernel_ref, arrived,
):
    kernel_copy = pltpu.make_async_copy(kernel_hbm, kernel_ref, arrived)
    kernel_copy.start()
    own_frames, _, cols, channels = attended_ref.shape
    frames, rows = resid.shape[:2]
    tokens = frames * rows * cols
    frame_tokens = rows * cols
    space = lax.axis_index("space")
    block = lax.axis_index("tm")
    half = lax.axis_index("chan")
    width = D // NGROUP
    count = tokens * width
    own_rows = pl.ds(pl.multiple_of(half * channels, channels), channels)
    other_rows = pl.ds(pl.multiple_of((1 - half) * channels, channels), channels)

    blocks = frames // own_frames

    def side_parts(near, far):
        pieces = []
        for ref in (near, far):
            pieces += [ref[at : at + own_frames * cols, :] for at in range(0, rows // 2 * frames * cols, own_frames * cols)]
        laid = []
        for index in range(blocks):
            for frame in range(own_frames):
                at = slice(frame * cols, (frame + 1) * cols)
                laid += [pieces[row * blocks + index][at] for row in range(rows)]
        parts = near[near.shape[0] - GAIN_ROWS : near.shape[0], :].astype(jnp.float32)
        gains = [parts[at : at + 1] + parts[at + 1 : at + 2] + parts[at + 2 : at + 3] for at in (0, 3)]
        return jnp.concatenate(laid, axis=0), *gains

    sides, first_gains, second_gains = zip(side_parts(near_ref, far_ref), side_parts(other_near_ref, other_far_ref))
    for side, gain in enumerate(first_gains):
        values = sides[side].astype(jnp.float32)
        centre, scale = moments(values, count)
        normed[side] = ((values - centre) * scale * gain).astype(jnp.bfloat16)

    for weight_ref, target in zip((query_ref, key_ref, value_ref), (queries, keyed, valued)):
        target[...] = (
            jnp.dot(normed[0], weight_ref[own_rows, :], preferred_element_type=jnp.float32)
            + jnp.dot(normed[1], weight_ref[other_rows, :], preferred_element_type=jnp.float32)
        ).astype(jnp.bfloat16)

    in_channels = kernel_ref.shape[3]
    in_cols = pl.ds(pl.multiple_of(block * in_channels, in_channels), in_channels)
    own_cols = pl.ds(pl.multiple_of(half * channels, channels), channels)
    mine_in = block == half
    for frame in range(frames):
        at = slice(frame * frame_tokens, (frame + 1) * frame_tokens)
        scores = lax.dot_general(
            queries[at, :], keyed[at, :], (((1,), (1,)), ((), ())), preferred_element_type=jnp.float32
        ) * (D ** (-0.5))
        weights = jnp.exp(scores - jnp.max(scores, axis=1, keepdims=True))
        mass = jnp.sum(weights, axis=1, keepdims=True)
        mixed = jnp.dot(weights.astype(jnp.bfloat16), valued[at, :], preferred_element_type=jnp.float32)
        mixed = (mixed / mass).astype(jnp.bfloat16)
        if frame < own_frames:
            attended_ref[frame, 0] = jnp.dot(
                mixed[:cols], out_weight_ref[:, own_cols], preferred_element_type=jnp.float32
            ).astype(jnp.bfloat16)
        projected = jnp.dot(
            mixed, out_weight_ref[:, in_cols], preferred_element_type=jnp.float32
        ).astype(jnp.bfloat16)
        source = jnp.where(mine_in, sides[0][at].astype(jnp.float32), sides[1][at].astype(jnp.float32))
        resid[frame] = (source + projected.astype(jnp.float32)).reshape(rows, cols, in_channels)

    centre, scale = moments(resid[...].reshape(tokens, in_channels), count)
    gain = jnp.where(mine_in, *second_gains)
    for tap in range(3):
        row = space + (tap - 1)
        inside = jnp.logical_and(row >= 0, row < rows)
        place = jnp.where(inside, space ^ row, 0)
        for frame in range(frames):
            relative = ((frame // own_frames) ^ block) * own_frames + frame % own_frames
            values = (resid[relative, place] - centre) * scale * gain
            values = values / (1.0 + jnp.exp(-values))
            activated[tap, frame] = jnp.where(inside, values, 0.0).astype(jnp.bfloat16)

    out_channels = kernel_ref.shape[4]
    columns = [None] * 3
    kernel_copy.wait()
    for col_tap in range(3):
        total = None
        for time_tap in (2, 1, 0):
            late = 2 - time_tap
            shorter = None
            for row_tap in range(3):
                window = activated[row_tap, 0 : frames - late].reshape((frames - late) * cols, in_channels)
                term = jnp.dot(window, kernel_ref[time_tap, row_tap, col_tap], preferred_element_type=jnp.float32)
                shorter = term if shorter is None else shorter + term
            if late:
                shorter = jnp.concatenate([jnp.zeros((late * cols, out_channels), jnp.float32), shorter], axis=0)
            total = shorter if total is None else total + shorter
        columns[col_tap] = total
    place = lax.broadcasted_iota(jnp.int32, (frames * cols, out_channels), 0) % cols
    left = jnp.where(place == 0, 0.0, pltpu.roll(columns[0], 1, 0))
    right = jnp.where(place == cols - 1, 0.0, pltpu.roll(columns[2], frames * cols - 1, 0))
    summed = (columns[1] + left + right).reshape(frames, cols, out_channels)
    for index in range(blocks):
        piece = summed[index * own_frames : (index + 1) * own_frames]

        @pl.when(index == block)
        def _():
            keep_ref[...] = piece

        @pl.when(index != block)
        def _():
            send_ref[(index ^ block) - 1] = piece.astype(jnp.bfloat16)


def gathered_plan(
    hidden_states, first_gain, second_gain, query_weight, key_weight, value_weight, out_weight, conv_kernel
):
    frames, _, cols, channels = hidden_states.shape
    rows, blocks = lax.axis_size("space"), lax.axis_size("tm")
    own = hidden_states.reshape(frames * cols, channels)
    gains = (first_gain.reshape(1, channels), second_gain.reshape(1, channels))
    far_own = {row: exchange(own, "space", row) for row in range(rows - 1, rows // 2 - 1, -1)}
    near = [exchange(own, ("space", "tm"), step) for step in range(1, rows // 2 * blocks)]
    far = []
    for row in range(rows // 2, rows):
        far += [far_own[row]] + [exchange(far_own[row], "tm", step) for step in range(1, blocks)]
    near_mine = pack_near(near, own, gains)
    near_other = exchange(near_mine, "chan", 1)
    far_mine = pack_far(far)
    far_other = exchange(far_mine, "chan", 1)
    out_channels = conv_kernel.shape[4]
    in_channels = conv_kernel.shape[3]
    tokens = blocks * frames * rows * cols
    weights = stage((query_weight, key_weight, value_weight, out_weight))
    attended, keep, send = pl.pallas_call(
        main_kernel,
        out_shape=(
            jax.ShapeDtypeStruct((frames, 1, cols, channels), jnp.bfloat16),
            jax.ShapeDtypeStruct((frames, cols, out_channels), jnp.float32),
            jax.ShapeDtypeStruct((blocks - 1, frames, cols, out_channels), jnp.bfloat16),
        ),
        scratch_shapes=[
            pltpu.VMEM((2, tokens, channels), jnp.bfloat16),
            pltpu.VMEM((tokens, D), jnp.bfloat16),
            pltpu.VMEM((tokens, D), jnp.bfloat16),
            pltpu.VMEM((tokens, D), jnp.bfloat16),
            pltpu.VMEM((blocks * frames, rows, cols, in_channels), jnp.float32),
            pltpu.VMEM((3, blocks * frames, cols, in_channels), jnp.bfloat16),
            pltpu.VMEM(conv_kernel.shape, conv_kernel.dtype),
            pltpu.SemaphoreType.DMA,
        ],
        in_specs=[pl.BlockSpec(memory_space=pltpu.VMEM)] * 8 + [pl.BlockSpec(memory_space=pltpu.HBM)],
        compiler_params=pltpu.CompilerParams(vmem_limit_bytes=24 * 1024 * 1024),
        name="block",
    )(near_mine, far_mine, near_other, far_other, *weights, in_hbm(conv_kernel))
    total = keep
    for step in range(1, blocks):
        total = total + exchange(send[step - 1], "tm", step).astype(jnp.float32)
    return attended, total.astype(jnp.bfloat16).reshape(frames, 1, cols, out_channels)


def power_of_two(count):
    return count & (count - 1) == 0


def on_device(hidden_states, *others):
    frames, rows, cols, channels = hidden_states.shape
    spaces, blocks = lax.axis_size("space"), lax.axis_size("tm")
    tokens = frames * blocks * spaces * rows * cols
    fits = tokens * D <= 2 ** 20 and rows == 1 and lax.axis_size("chan") == 2 and blocks == 2
    if fits and power_of_two(spaces):
        return gathered_plan(hidden_states, *others)
    return split_plan(hidden_states, *others)


def solution(mesh):
    placed = (
        P(("groups", "tm"), "space", None, "chan"),
        P("chan"),
        P("chan"),
        P(),
        P(),
        P(),
        P(),
        P(None, None, None, "tm", "chan"),
    )
    return jax.shard_map(
        on_device,
        mesh=mesh,
        in_specs=placed,
        out_specs=(
            P(("groups", "tm"), "space", None, "chan"),
            P(("groups", "tm"), "space", None, "chan"),
        ),
        check_vma=False,
    )
```

```python
import functools

import jax
import jax.numpy as jnp
from jax import lax
from jax.experimental import pallas as pl
from jax.experimental.pallas import tpu as pltpu
from jax.sharding import PartitionSpec as P

D = 512
NGROUP = 32


EPSILON = 1e-06


def shifted_2(x, axis, by):
    peers = lax.axis_size(axis)
    pairs = [(i, i + by) for i in range(peers) if 0 <= i + by < peers]
    return lax.ppermute(x, axis, pairs)


def padded_2(cells, sides, width):
    for axis, dim in sides:
        count = lax.axis_size(axis)
        ends = count - 1
        head = lax.slice_in_dim(cells, 0, width, axis=dim)
        tail = lax.slice_in_dim(cells, cells.shape[dim] - width, cells.shape[dim], axis=dim)
        cells = jnp.concatenate(
            [
                lax.ppermute(tail, axis, [(i, (i + 1) % count) for i in range(ends)]),
                cells,
                lax.ppermute(head, axis, [((i + 1) % count, i) for i in range(ends)]),
            ],
            axis=dim,
        )
    return cells


def normalize(source, gain_vector):
    channels = source.shape[3]
    group_width = D // NGROUP
    grouped = source.reshape(-1, channels // group_width, group_width)
    population = grouped.shape[0] * group_width * lax.axis_size("space") * lax.axis_size("tm")
    group_sums, group_squares = lax.psum(
        (jnp.sum(grouped, axis=(0, 2)), jnp.sum(grouped * grouped, axis=(0, 2))), ("space", "tm")
    )
    centre = group_sums / population
    spread = jnp.maximum(group_squares / population - centre * centre, 0.0)
    shifted = grouped - centre[None, :, None]
    scaled = shifted * lax.rsqrt(spread + EPSILON)[None, :, None]
    return scaled.reshape(source.shape) * gain_vector


def attend(normed, query_weight, key_weight, value_weight, out_weight):
    frame_count, row_count, col_count, channels = normed.shape
    token_count = frame_count * row_count * col_count
    tokens = normed.reshape(token_count, channels)
    halves = lax.all_to_all(tokens, "chan", split_axis=0, concat_axis=1, tiled=True)
    half_rows = halves.shape[0]
    queries = jnp.dot(halves, query_weight, preferred_element_type=jnp.float32).astype(jnp.bfloat16)
    keyed = jnp.dot(halves, key_weight, preferred_element_type=jnp.float32).astype(jnp.bfloat16)
    valued = jnp.dot(halves, value_weight, preferred_element_type=jnp.float32).astype(jnp.bfloat16)
    score_scale = D ** (-0.5)
    running_max = jnp.full((half_rows,), -1e30, jnp.float32)
    key_piece = lax.all_gather(keyed, "space", axis=0, tiled=True)
    value_piece = lax.all_gather(valued, "space", axis=0, tiled=True)
    scores = jnp.dot(queries, key_piece.T, preferred_element_type=jnp.float32) * score_scale
    newest_max = jnp.maximum(running_max, jnp.max(scores, axis=1))
    weights = jnp.exp(scores - newest_max[:, None])
    running_sum = jnp.sum(weights, axis=1)
    accumulated = jnp.dot(
        weights.astype(jnp.bfloat16), value_piece, preferred_element_type=jnp.float32
    )
    mixed = (accumulated / running_sum[:, None]).astype(jnp.bfloat16)
    projected = jnp.dot(mixed, out_weight, preferred_element_type=jnp.float32).astype(jnp.bfloat16)
    returned = lax.all_to_all(projected, "chan", split_axis=1, concat_axis=0, tiled=True)
    return returned.reshape(frame_count, row_count, col_count, channels)


def join_channels(activated):
    return lax.all_gather(activated, "chan", axis=3, tiled=True)


def extend(frames_in):
    earlier = shifted_2(frames_in, "tm", 1)
    timed = jnp.concatenate([earlier, frames_in], axis=0)
    rimmed = padded_2(timed, (("space", 1),), 1)
    return jnp.pad(rimmed, ((0, 0), (0, 0), (1, 1), (0, 0)))


def convolve(activated, conv_kernel):
    frame_count, row_count, col_count = (activated.shape[0], activated.shape[1], activated.shape[2])
    padded = extend(join_channels(activated))
    out_width = conv_kernel.shape[4]
    initial = jnp.zeros((frame_count * row_count * col_count, out_width), jnp.float32)
    running_total = initial
    piece = lax.all_gather(conv_kernel, "tm", axis=3, tiled=True)
    for time_tap in range(3):
        for row_tap in range(3):
            for col_tap in range(3):
                window = padded[
                    time_tap : time_tap + frame_count,
                    row_tap : row_tap + row_count,
                    col_tap : col_tap + col_count,
                ]
                window = window.reshape(frame_count * row_count * col_count, piece.shape[3])
                running_total = running_total + jnp.dot(
                    window, piece[time_tap, row_tap, col_tap], preferred_element_type=jnp.float32
                )
    return running_total.reshape(frame_count, row_count, col_count, out_width).astype(jnp.bfloat16)


def split_plan(
    hidden_states,
    first_gain,
    second_gain,
    query_weight,
    key_weight,
    value_weight,
    out_weight,
    conv_kernel,
):
    source = hidden_states.astype(jnp.float32)
    normed = normalize(source, first_gain).astype(jnp.bfloat16)
    attended = attend(normed, query_weight, key_weight, value_weight, out_weight)
    resid = source + attended.astype(jnp.float32)
    activated = jax.nn.silu(normalize(resid, second_gain)).astype(jnp.bfloat16)
    convolved = convolve(activated, conv_kernel)
    return (attended, convolved)


GAIN_ROWS = 16


def exchange(x, axes, step):
    peers = lax.axis_size(axes)
    return lax.ppermute(x, axes, [(i, i ^ step) for i in range(peers)])


def stage_kernel(*refs):
    count = len(refs) // 2 - 1
    copies = [pltpu.make_async_copy(refs[i], refs[count + 1 + i], refs[-1].at[i]) for i in range(count)]
    for copy in copies:
        copy.start()
    for copy in copies:
        copy.wait()


def stage(arrays, after):
    return pl.pallas_call(
        stage_kernel,
        out_shape=tuple(jax.ShapeDtypeStruct(array.shape, array.dtype) for array in arrays),
        in_specs=[pl.BlockSpec(memory_space=pltpu.HBM)] * len(arrays) + [pl.BlockSpec(memory_space=pl.ANY)],
        out_specs=tuple(pl.BlockSpec(memory_space=pltpu.VMEM) for _ in arrays),
        scratch_shapes=[pltpu.SemaphoreType.DMA((len(arrays),))],
        compiler_params=pltpu.CompilerParams(vmem_limit_bytes=1 << 20),
        name="stage",
    )(*(in_hbm(array) for array in arrays), after)


def pack_kernel(*refs):
    end = 0
    for piece_ref in refs[:-1]:
        start, end = end, end + piece_ref.shape[0]
        refs[-1][start:end, :] = piece_ref[...]


def near_kernel(first_ref, second_ref, *refs):
    pack_kernel(*refs)
    parts = split_parts(first_ref[...]) + split_parts(second_ref[...])
    parts = [part.astype(jnp.float32) for part in parts]
    parts.append(jnp.zeros((GAIN_ROWS - len(parts), first_ref.shape[1]), jnp.float32))
    end = refs[-1].shape[0]
    refs[-1][end - GAIN_ROWS : end, :] = jnp.concatenate(parts, axis=0).astype(jnp.bfloat16)


def pack(kernel, pieces, name, gains=()):
    size = sum(piece.shape[0] for piece in pieces) + (GAIN_ROWS if gains else 0)
    return pl.pallas_call(
        kernel,
        out_shape=jax.ShapeDtypeStruct((size, pieces[0].shape[1]), pieces[0].dtype),
        compiler_params=pltpu.CompilerParams(vmem_limit_bytes=2 * 1024 * 1024),
        name=name,
    )(*gains, *pieces)


def in_hbm(array):
    return pltpu.with_memory_space_constraint(array, pltpu.HBM)


def split_parts(values):
    parts = []
    for _ in range(3):
        rounded = values.astype(jnp.bfloat16)
        parts.append(rounded)
        values = values - rounded.astype(jnp.float32)
    return parts


def channel_sums(values):
    tokens, channels = values.shape
    parts = values.reshape(tokens // 8, 8, channels)
    return [jnp.sum(jnp.sum(part, axis=0), axis=0, keepdims=True) for part in (parts, parts * parts)]


def group_statistics(rows, count):
    channels = rows[0].shape[1]
    width = D // NGROUP
    left = lax.broadcasted_iota(jnp.int32, (channels, channels), 0) // width
    right = lax.broadcasted_iota(jnp.int32, (channels, channels), 1) // width
    member = jnp.where(left == right, 1.0, 0.0).astype(jnp.bfloat16)
    parts = [part for row in rows for part in split_parts(row)]
    parts += [jnp.zeros((1, channels), jnp.bfloat16)] * (16 - len(parts))
    totals = jnp.dot(jnp.concatenate(parts, axis=0), member, preferred_element_type=jnp.float32)
    means = [
        (totals[at : at + 1] + totals[at + 1 : at + 2] + totals[at + 2 : at + 3]) * (1.0 / count)
        for at in range(0, 3 * len(rows), 3)
    ]
    found = []
    for centre, square in zip(means[::2], means[1::2]):
        spread = jnp.maximum(square - centre * centre, 0.0)
        found.append((centre, lax.rsqrt(spread + EPSILON)))
    return found


def main_kernel(
    near_ref, far_ref, other_near_ref, other_far_ref, query_ref, key_ref, value_ref, out_weight_ref, kernel_hbm,
    attended_ref, activated, send_ref, kernel_ref,
    normed, queries, keyed, valued, mixed, resid, arrived,
):
    kernel_copy = pltpu.make_async_copy(kernel_hbm, kernel_ref, arrived)
    kernel_copy.start()
    own_frames, _, cols, channels = attended_ref.shape
    frames, rows = resid.shape[:2]
    tokens = frames * rows * cols
    frame_tokens = rows * cols
    space = lax.axis_index("space")
    block = lax.axis_index("tm")
    half = lax.axis_index("chan")
    width = D // NGROUP
    count = tokens * width
    own_rows = pl.ds(pl.multiple_of(half * channels, channels), channels)
    other_rows = pl.ds(pl.multiple_of((1 - half) * channels, channels), channels)

    blocks = frames // own_frames

    def side_parts(near, far):
        size = own_frames * cols
        pieces = [ref[at : at + size, :] for ref in (near, far) for at in range(0, ref.shape[0] - size + 1, size)]
        laid = []
        for index in range(blocks):
            for frame in range(own_frames):
                at = slice(frame * cols, (frame + 1) * cols)
                laid += [pieces[row * blocks + index][at] for row in range(rows)]
        parts = near[near.shape[0] - GAIN_ROWS : near.shape[0], :].astype(jnp.float32)
        gains = [parts[at : at + 1] + parts[at + 1 : at + 2] + parts[at + 2 : at + 3] for at in (0, 3)]
        return jnp.concatenate(laid, axis=0), *gains

    sides, first_gains, second_gains = zip(side_parts(near_ref, far_ref), side_parts(other_near_ref, other_far_ref))
    statistics = group_statistics(
        channel_sums(sides[0].astype(jnp.float32)) + channel_sums(sides[1].astype(jnp.float32)), count
    )
    for side, gain in enumerate(first_gains):
        centre, scale = statistics[side]
        normed[side] = ((sides[side].astype(jnp.float32) - centre) * (scale * gain)).astype(jnp.bfloat16)

    for weight_ref, target in zip((query_ref, key_ref, value_ref), (queries, keyed, valued)):
        target[...] = (
            jnp.dot(normed[0], weight_ref[own_rows, :], preferred_element_type=jnp.float32)
            + jnp.dot(normed[1], weight_ref[other_rows, :], preferred_element_type=jnp.float32)
        ).astype(jnp.bfloat16)

    in_channels = kernel_ref.shape[3]
    in_cols = pl.ds(pl.multiple_of(block * in_channels, in_channels), in_channels)
    own_cols = pl.ds(pl.multiple_of(half * channels, channels), channels)
    mine_in = block == half
    spans = [slice(frame * frame_tokens, (frame + 1) * frame_tokens) for frame in range(frames)]
    scores = [
        lax.dot_general(queries[at, :], keyed[at, :], (((1,), (1,)), ((), ())), preferred_element_type=jnp.float32)
        for at in spans
    ]
    for at, score in zip(spans, scores):
        peak = jnp.max(score, axis=1, keepdims=True)
        weights = jnp.exp((score - peak) * (D ** (-0.5)))
        mass = jnp.sum(weights, axis=1, keepdims=True)
        blend = jnp.dot(weights.astype(jnp.bfloat16), valued[at, :], preferred_element_type=jnp.float32)
        mixed[at, :] = (blend * (1.0 / mass)).astype(jnp.bfloat16)
    projected = jnp.dot(
        mixed[...], out_weight_ref[:, in_cols], preferred_element_type=jnp.float32
    ).astype(jnp.bfloat16)
    source = jnp.where(mine_in, sides[0].astype(jnp.float32), sides[1].astype(jnp.float32))
    total = source + projected.astype(jnp.float32)
    resid[...] = total.reshape(frames, rows, cols, in_channels)
    own_mixed = jnp.concatenate([mixed[at.start : at.start + cols, :] for at in spans[:own_frames]], axis=0)
    attended_ref[...] = jnp.dot(
        own_mixed, out_weight_ref[:, own_cols], preferred_element_type=jnp.float32
    ).astype(jnp.bfloat16).reshape(own_frames, 1, cols, channels)

    kernel_copy.wait()
    ((centre, scale),) = group_statistics(channel_sums(total), count)
    scale = scale * jnp.where(mine_in, *second_gains)
    activated[:, 0:2] = jnp.zeros((3, 2, cols, in_channels), jnp.bfloat16)
    for tap in range(3):
        row = space + (tap - 1)
        inside = jnp.logical_and(row >= 0, row < rows)
        place = jnp.where(inside, space ^ row, 0)
        for frame in range(frames):
            relative = ((frame // own_frames) ^ block) * own_frames + frame % own_frames
            values = (resid[relative, place] - centre) * scale
            values = 0.5 * values * (1.0 + jnp.tanh(0.5 * values))
            activated[tap, frame + 2] = jnp.where(inside, values, 0.0).astype(jnp.bfloat16)

    send_ref[...] = partial_conv(activated, kernel_ref, 1 - block, own_frames).astype(jnp.bfloat16)


def partial_conv(activated, kernel_ref, block, frames):
    cols, in_channels = activated.shape[2:]
    tokens = frames * cols
    columns = []
    for col_tap in range(3):
        total = None
        for time_tap in range(3):
            for row_tap in range(3):
                window = activated[row_tap, pl.ds(block * frames + time_tap, frames)].reshape(tokens, in_channels)
                term = jnp.dot(window, kernel_ref[time_tap, row_tap, col_tap], preferred_element_type=jnp.float32)
                total = term if total is None else total + term
        columns.append(total)
    place = lax.broadcasted_iota(jnp.int32, columns[0].shape, 0) % cols
    left = jnp.where(place == 0, 0.0, pltpu.roll(columns[0], 1, 0))
    right = jnp.where(place == cols - 1, 0.0, pltpu.roll(columns[2], tokens - 1, 0))
    return columns[1] + left + right


def own_kernel(activated, kernel_ref, attended_ref, attended_hbm, keep_ref, sent):
    copy = pltpu.make_async_copy(attended_ref, attended_hbm, sent)
    copy.start()
    keep_ref[...] = partial_conv(activated, kernel_ref, lax.axis_index("tm"), attended_ref.shape[0])
    copy.wait()


def gathered_plan(
    hidden_states, first_gain, second_gain, query_weight, key_weight, value_weight, out_weight, conv_kernel
):
    frames, _, cols, channels = hidden_states.shape
    rows, blocks = lax.axis_size("space"), lax.axis_size("tm")
    own = hidden_states.reshape(frames * cols, channels)
    gains = (first_gain.reshape(1, channels), second_gain.reshape(1, channels))
    by_row = {row: exchange(own, "space", row) for row in range(rows - 1, 0, -1)}
    first = exchange(own, "tm", 1)
    onward = {row: exchange(piece, "tm", 1) for row, piece in by_row.items() if row >= rows // 2}
    for row in range(1, rows // 2):
        onward[row] = exchange(own, ("space", "tm"), row * blocks + 1)
    *weights, own_staged, first_gain, second_gain = stage(
        (query_weight, key_weight, value_weight, out_weight, own, *gains), by_row[rows // 2]
    )
    near = [own_staged, first]
    for row in range(1, rows // 2):
        near += [by_row[row], onward[row]]
    far = [piece for row in range(rows // 2, rows) for piece in (by_row[row], onward[row])]
    near_mine = pack(near_kernel, near, "near", (first_gain, second_gain))
    near_other = exchange(near_mine, "chan", 1)
    far_mine = pack(pack_kernel, far, "far")
    far_other = exchange(far_mine, "chan", 1)
    in_channels, out_channels = conv_kernel.shape[3:]
    tokens = blocks * frames * rows * cols
    in_vmem = pl.BlockSpec(memory_space=pltpu.VMEM)
    attended, activated, send, kernel = pl.pallas_call(
        main_kernel,
        out_shape=(
            jax.ShapeDtypeStruct((frames, 1, cols, channels), jnp.bfloat16),
            jax.ShapeDtypeStruct((3, blocks * frames + 2, cols, in_channels), jnp.bfloat16),
            jax.ShapeDtypeStruct((frames * cols, out_channels), jnp.bfloat16),
            jax.ShapeDtypeStruct(conv_kernel.shape, conv_kernel.dtype),
        ),
        in_specs=[in_vmem] * 8 + [pl.BlockSpec(memory_space=pltpu.HBM)],
        out_specs=(in_vmem,) * 4,
        scratch_shapes=[pltpu.VMEM((2, tokens, channels), jnp.bfloat16)]
        + [pltpu.VMEM((tokens, D), jnp.bfloat16)] * 4
        + [pltpu.VMEM((blocks * frames, rows, cols, in_channels), jnp.float32), pltpu.SemaphoreType.DMA],
        compiler_params=pltpu.CompilerParams(vmem_limit_bytes=24 * 1024 * 1024),
        name="block",
    )(near_mine, far_mine, near_other, far_other, *weights, in_hbm(conv_kernel))
    received = exchange(send, "tm", 1)
    attended, keep = pl.pallas_call(
        own_kernel,
        out_shape=(
            jax.ShapeDtypeStruct(attended.shape, attended.dtype),
            jax.ShapeDtypeStruct((frames * cols, out_channels), jnp.float32),
        ),
        in_specs=[in_vmem] * 3,
        out_specs=(pl.BlockSpec(memory_space=pl.ANY), in_vmem),
        scratch_shapes=[pltpu.SemaphoreType.DMA],
        compiler_params=pltpu.CompilerParams(vmem_limit_bytes=4 * 1024 * 1024),
        name="own",
    )(activated, kernel, attended)
    total = keep + received.astype(jnp.float32)
    return attended, total.astype(jnp.bfloat16).reshape(frames, 1, cols, out_channels)


def power_of_two(count):
    return count & (count - 1) == 0


def on_device(hidden_states, *others):
    frames, rows, cols, channels = hidden_states.shape
    spaces, blocks = lax.axis_size("space"), lax.axis_size("tm")
    tokens = frames * blocks * spaces * rows * cols
    fits = tokens * D <= 2 ** 20 and rows == 1 and lax.axis_size("chan") == 2 and blocks == 2
    if fits and power_of_two(spaces):
        return gathered_plan(hidden_states, *others)
    return split_plan(hidden_states, *others)


def solution(mesh):
    placed = (
        P(("groups", "tm"), "space", None, "chan"),
        P("chan"),
        P("chan"),
        P(),
        P(),
        P(),
        P(),
        P(None, None, None, "tm", "chan"),
    )
    return jax.shard_map(
        on_device,
        mesh=mesh,
        in_specs=placed,
        out_specs=(
            P(("groups", "tm"), "space", None, "chan"),
            P(("groups", "tm"), "space", None, "chan"),
        ),
        check_vma=False,
    )
```

```python
import functools

import jax
import jax.numpy as jnp
from jax import lax
from jax.experimental import pallas as pl
from jax.experimental.pallas import tpu as pltpu
from jax.sharding import PartitionSpec as P

D = 512
NGROUP = 32


EPSILON = 1e-06


def shifted_2(x, axis, by):
    peers = lax.axis_size(axis)
    pairs = [(i, i + by) for i in range(peers) if 0 <= i + by < peers]
    return lax.ppermute(x, axis, pairs)


def padded_2(cells, sides, width):
    for axis, dim in sides:
        count = lax.axis_size(axis)
        ends = count - 1
        head = lax.slice_in_dim(cells, 0, width, axis=dim)
        tail = lax.slice_in_dim(cells, cells.shape[dim] - width, cells.shape[dim], axis=dim)
        cells = jnp.concatenate(
            [
                lax.ppermute(tail, axis, [(i, (i + 1) % count) for i in range(ends)]),
                cells,
                lax.ppermute(head, axis, [((i + 1) % count, i) for i in range(ends)]),
            ],
            axis=dim,
        )
    return cells


def normalize(source, gain_vector):
    channels = source.shape[3]
    group_width = D // NGROUP
    grouped = source.reshape(-1, channels // group_width, group_width)
    population = grouped.shape[0] * group_width * lax.axis_size("space") * lax.axis_size("tm")
    group_sums, group_squares = lax.psum(
        (jnp.sum(grouped, axis=(0, 2)), jnp.sum(grouped * grouped, axis=(0, 2))), ("space", "tm")
    )
    centre = group_sums / population
    spread = jnp.maximum(group_squares / population - centre * centre, 0.0)
    shifted = grouped - centre[None, :, None]
    scaled = shifted * lax.rsqrt(spread + EPSILON)[None, :, None]
    return scaled.reshape(source.shape) * gain_vector


def attend(normed, query_weight, key_weight, value_weight, out_weight):
    frame_count, row_count, col_count, channels = normed.shape
    token_count = frame_count * row_count * col_count
    tokens = normed.reshape(token_count, channels)
    halves = lax.all_to_all(tokens, "chan", split_axis=0, concat_axis=1, tiled=True)
    half_rows = halves.shape[0]
    queries = jnp.dot(halves, query_weight, preferred_element_type=jnp.float32).astype(jnp.bfloat16)
    keyed = jnp.dot(halves, key_weight, preferred_element_type=jnp.float32).astype(jnp.bfloat16)
    valued = jnp.dot(halves, value_weight, preferred_element_type=jnp.float32).astype(jnp.bfloat16)
    score_scale = D ** (-0.5)
    running_max = jnp.full((half_rows,), -1e30, jnp.float32)
    key_piece = lax.all_gather(keyed, "space", axis=0, tiled=True)
    value_piece = lax.all_gather(valued, "space", axis=0, tiled=True)
    scores = jnp.dot(queries, key_piece.T, preferred_element_type=jnp.float32) * score_scale
    newest_max = jnp.maximum(running_max, jnp.max(scores, axis=1))
    weights = jnp.exp(scores - newest_max[:, None])
    running_sum = jnp.sum(weights, axis=1)
    accumulated = jnp.dot(
        weights.astype(jnp.bfloat16), value_piece, preferred_element_type=jnp.float32
    )
    mixed = (accumulated / running_sum[:, None]).astype(jnp.bfloat16)
    projected = jnp.dot(mixed, out_weight, preferred_element_type=jnp.float32).astype(jnp.bfloat16)
    returned = lax.all_to_all(projected, "chan", split_axis=1, concat_axis=0, tiled=True)
    return returned.reshape(frame_count, row_count, col_count, channels)


def join_channels(activated):
    return lax.all_gather(activated, "chan", axis=3, tiled=True)


def extend(frames_in):
    earlier = shifted_2(frames_in, "tm", 1)
    timed = jnp.concatenate([earlier, frames_in], axis=0)
    rimmed = padded_2(timed, (("space", 1),), 1)
    return jnp.pad(rimmed, ((0, 0), (0, 0), (1, 1), (0, 0)))


def convolve(activated, conv_kernel):
    frame_count, row_count, col_count = (activated.shape[0], activated.shape[1], activated.shape[2])
    padded = extend(join_channels(activated))
    out_width = conv_kernel.shape[4]
    initial = jnp.zeros((frame_count * row_count * col_count, out_width), jnp.float32)
    running_total = initial
    piece = lax.all_gather(conv_kernel, "tm", axis=3, tiled=True)
    for time_tap in range(3):
        for row_tap in range(3):
            for col_tap in range(3):
                window = padded[
                    time_tap : time_tap + frame_count,
                    row_tap : row_tap + row_count,
                    col_tap : col_tap + col_count,
                ]
                window = window.reshape(frame_count * row_count * col_count, piece.shape[3])
                running_total = running_total + jnp.dot(
                    window, piece[time_tap, row_tap, col_tap], preferred_element_type=jnp.float32
                )
    return running_total.reshape(frame_count, row_count, col_count, out_width).astype(jnp.bfloat16)


def split_plan(
    hidden_states,
    first_gain,
    second_gain,
    query_weight,
    key_weight,
    value_weight,
    out_weight,
    conv_kernel,
):
    source = hidden_states.astype(jnp.float32)
    normed = normalize(source, first_gain).astype(jnp.bfloat16)
    attended = attend(normed, query_weight, key_weight, value_weight, out_weight)
    resid = source + attended.astype(jnp.float32)
    activated = jax.nn.silu(normalize(resid, second_gain)).astype(jnp.bfloat16)
    convolved = convolve(activated, conv_kernel)
    return (attended, convolved)


GAIN_ROWS = 16


def exchange(x, axes, step):
    peers = lax.axis_size(axes)
    return lax.ppermute(x, axes, [(i, i ^ step) for i in range(peers)])


def stage_kernel(*refs):
    count = len(refs) // 2 - 1
    targets = refs[count + 1 : -1]
    copies = [
        pltpu.make_async_copy(source.at[pl.ds(0, target.shape[0])], target, refs[-1].at[i])
        for i, (source, target) in enumerate(zip(refs, targets))
    ]
    for copy in copies:
        copy.start()
    for copy in copies:
        copy.wait()


def stage(arrays, sizes, after):
    return pl.pallas_call(
        stage_kernel,
        out_shape=tuple(
            jax.ShapeDtypeStruct((size, *array.shape[1:]), array.dtype) for array, size in zip(arrays, sizes)
        ),
        in_specs=[pl.BlockSpec(memory_space=pltpu.HBM)] * len(arrays) + [pl.BlockSpec(memory_space=pl.ANY)],
        out_specs=tuple(pl.BlockSpec(memory_space=pltpu.VMEM) for _ in arrays),
        scratch_shapes=[pltpu.SemaphoreType.DMA((len(arrays),))],
        compiler_params=pltpu.CompilerParams(vmem_limit_bytes=1 << 20),
        name="stage",
    )(*(in_hbm(array) for array in arrays), after)


def pack_kernel(*refs):
    end = 0
    for piece_ref in refs[:-1]:
        start, end = end, end + piece_ref.shape[0]
        refs[-1][start:end, :] = piece_ref[...]


def near_kernel(first_ref, second_ref, *refs):
    pack_kernel(*refs)
    parts = split_parts(first_ref[...]) + split_parts(second_ref[...])
    parts = [part.astype(jnp.float32) for part in parts]
    parts.append(jnp.zeros((GAIN_ROWS - len(parts), first_ref.shape[1]), jnp.float32))
    end = refs[-1].shape[0]
    refs[-1][end - GAIN_ROWS : end, :] = jnp.concatenate(parts, axis=0).astype(jnp.bfloat16)


def pack(kernel, pieces, name, gains=()):
    size = sum(piece.shape[0] for piece in pieces) + (GAIN_ROWS if gains else 0)
    return pl.pallas_call(
        kernel,
        out_shape=jax.ShapeDtypeStruct((size, pieces[0].shape[1]), pieces[0].dtype),
        compiler_params=pltpu.CompilerParams(vmem_limit_bytes=2 * 1024 * 1024),
        name=name,
    )(*gains, *pieces)


def in_hbm(array):
    return pltpu.with_memory_space_constraint(array, pltpu.HBM)


def split_parts(values):
    parts = []
    for _ in range(3):
        rounded = values.astype(jnp.bfloat16)
        parts.append(rounded)
        values = values - rounded.astype(jnp.float32)
    return parts


def channel_sums(values):
    tokens, channels = values.shape
    parts = values.reshape(tokens // 8, 8, channels)
    return [jnp.sum(jnp.sum(part, axis=0), axis=0, keepdims=True) for part in (parts, parts * parts)]


def group_statistics(rows, count):
    channels = rows[0].shape[1]
    width = D // NGROUP
    left = lax.broadcasted_iota(jnp.int32, (channels, channels), 0) // width
    right = lax.broadcasted_iota(jnp.int32, (channels, channels), 1) // width
    member = jnp.where(left == right, 1.0, 0.0).astype(jnp.bfloat16)
    parts = [part for row in rows for part in split_parts(row)]
    parts += [jnp.zeros((1, channels), jnp.bfloat16)] * (16 - len(parts))
    totals = jnp.dot(jnp.concatenate(parts, axis=0), member, preferred_element_type=jnp.float32)
    means = [
        (totals[at : at + 1] + totals[at + 1 : at + 2] + totals[at + 2 : at + 3]) * (1.0 / count)
        for at in range(0, 3 * len(rows), 3)
    ]
    found = []
    for centre, square in zip(means[::2], means[1::2]):
        spread = jnp.maximum(square - centre * centre, 0.0)
        found.append((centre, lax.rsqrt(spread + EPSILON)))
    return found


def core_tokens(near, far, layout):
    own_frames, cols, rows, blocks = layout
    size = own_frames * cols
    pieces = [ref[at : at + size, :] for ref in (near, far) for at in range(0, ref.shape[0] - size + 1, size)]
    laid = []
    for index in range(blocks):
        for frame in range(own_frames):
            at = slice(frame * cols, (frame + 1) * cols)
            laid += [pieces[row * blocks + index][at] for row in range(rows)]
    parts = near[near.shape[0] - GAIN_ROWS : near.shape[0], :].astype(jnp.float32)
    gains = [parts[at : at + 1] + parts[at + 1 : at + 2] + parts[at + 2 : at + 3] for at in (0, 3)]
    return jnp.concatenate(laid, axis=0), *gains


def normed_tokens(tokens, gain):
    values = tokens.astype(jnp.float32)
    ((centre, scale),) = group_statistics(channel_sums(values), tokens.shape[0] * (D // NGROUP))
    return ((values - centre) * (scale * gain)).astype(jnp.bfloat16)


def mine_kernel(
    near_ref, far_ref, query_ref, key_ref, value_ref, kernel_hbm,
    begun_query, begun_key, begun_value, early_ref, normed, arrived, *, layout,
):
    copy = pltpu.make_async_copy(kernel_hbm.at[pl.ds(1, early_ref.shape[0])], early_ref, arrived)
    copy.start()
    tokens, gain, _ = core_tokens(near_ref, far_ref, layout)
    normed[...] = normed_tokens(tokens, gain)
    channels = normed.shape[1]
    rows = pl.ds(pl.multiple_of(lax.axis_index("chan") * channels, channels), channels)
    for weight_ref, target in zip((query_ref, key_ref, value_ref), (begun_query, begun_key, begun_value)):
        target[...] = jnp.dot(normed[...], weight_ref[rows, :], preferred_element_type=jnp.float32)
    copy.wait()


def main_kernel(
    near_ref, far_ref, other_near_ref, other_far_ref, query_ref, key_ref, value_ref, begun_query, begun_key, begun_value,
    out_weight_ref, first_tap, second_tap, kernel_hbm,
    attended_ref, activated, send_ref, last_tap,
    normed, queries, keyed, valued, mixed, resid, arrived,
):
    kernel_copy = pltpu.make_async_copy(kernel_hbm.at[pl.ds(2, 1)], last_tap, arrived)
    kernel_copy.start()
    own_frames, _, cols, channels = attended_ref.shape
    frames, rows = resid.shape[:2]
    tokens = frames * rows * cols
    frame_tokens = rows * cols
    space = lax.axis_index("space")
    block = lax.axis_index("tm")
    half = lax.axis_index("chan")
    width = D // NGROUP
    count = tokens * width
    other_rows = pl.ds(pl.multiple_of((1 - half) * channels, channels), channels)

    blocks = frames // own_frames

    layout = (own_frames, cols, rows, blocks)
    sides, first_gains, second_gains = zip(
        core_tokens(near_ref, far_ref, layout), core_tokens(other_near_ref, other_far_ref, layout)
    )
    normed[...] = normed_tokens(sides[1], first_gains[1])
    for weight_ref, begun_ref, target in zip(
        (query_ref, key_ref, value_ref), (begun_query, begun_key, begun_value), (queries, keyed, valued)
    ):
        term = jnp.dot(normed[...], weight_ref[other_rows, :], preferred_element_type=jnp.float32)
        target[...] = (begun_ref[...] + term).astype(jnp.bfloat16)

    in_channels = first_tap.shape[3]
    in_cols = pl.ds(pl.multiple_of(block * in_channels, in_channels), in_channels)
    own_cols = pl.ds(pl.multiple_of(half * channels, channels), channels)
    mine_in = block == half
    spans = [slice(frame * frame_tokens, (frame + 1) * frame_tokens) for frame in range(frames)]
    scores = [
        lax.dot_general(queries[at, :], keyed[at, :], (((1,), (1,)), ((), ())), preferred_element_type=jnp.float32)
        for at in spans
    ]
    for at, score in zip(spans, scores):
        peak = jnp.max(score, axis=1, keepdims=True)
        weights = jnp.exp((score - peak) * (D ** (-0.5)))
        mass = jnp.sum(weights, axis=1, keepdims=True)
        blend = jnp.dot(weights.astype(jnp.bfloat16), valued[at, :], preferred_element_type=jnp.float32)
        mixed[at, :] = (blend * (1.0 / mass)).astype(jnp.bfloat16)
    projected = jnp.dot(
        mixed[...], out_weight_ref[:, in_cols], preferred_element_type=jnp.float32
    ).astype(jnp.bfloat16)
    source = jnp.where(mine_in, sides[0], sides[1])
    total = source.astype(jnp.float32) + projected.astype(jnp.float32)
    resid[...] = total.reshape(frames, rows, cols, in_channels)
    own_mixed = jnp.concatenate([mixed[at.start : at.start + cols, :] for at in spans[:own_frames]], axis=0)
    attended_ref[...] = jnp.dot(
        own_mixed, out_weight_ref[:, own_cols], preferred_element_type=jnp.float32
    ).astype(jnp.bfloat16).reshape(own_frames, 1, cols, channels)

    kernel_copy.wait()
    ((centre, scale),) = group_statistics(channel_sums(total), count)
    scale = scale * jnp.where(mine_in, *second_gains)
    activated[:, 0:2] = jnp.zeros((3, 2, cols, in_channels), jnp.bfloat16)
    for tap in range(3):
        row = space + (tap - 1)
        inside = jnp.logical_and(row >= 0, row < rows)
        place = jnp.where(inside, space ^ row, 0)
        for frame in range(frames):
            relative = ((frame // own_frames) ^ block) * own_frames + frame % own_frames
            values = (resid[relative, place] - centre) * scale
            values = 0.5 * values * (1.0 + jnp.tanh(0.5 * values))
            activated[tap, frame + 2] = jnp.where(inside, values, 0.0).astype(jnp.bfloat16)

    send_ref[...] = partial_conv(activated, (first_tap, second_tap, last_tap), 1 - block, own_frames).astype(jnp.bfloat16)


def partial_conv(activated, taps, block, frames):
    cols, in_channels = activated.shape[2:]
    tokens = frames * cols
    columns = []
    for col_tap in range(3):
        total = None
        for time_tap in range(3):
            for row_tap in range(3):
                window = activated[row_tap, pl.ds(block * frames + time_tap, frames)].reshape(tokens, in_channels)
                term = jnp.dot(window, taps[time_tap][0, row_tap, col_tap], preferred_element_type=jnp.float32)
                total = term if total is None else total + term
        columns.append(total)
    place = lax.broadcasted_iota(jnp.int32, columns[0].shape, 0) % cols
    left = jnp.where(place == 0, 0.0, pltpu.roll(columns[0], 1, 0))
    right = jnp.where(place == cols - 1, 0.0, pltpu.roll(columns[2], tokens - 1, 0))
    return columns[1] + left + right


def own_kernel(activated, first_tap, second_tap, last_tap, attended_ref, attended_hbm, keep_ref, sent):
    copy = pltpu.make_async_copy(attended_ref, attended_hbm, sent)
    copy.start()
    keep_ref[...] = partial_conv(activated, (first_tap, second_tap, last_tap), lax.axis_index("tm"), attended_ref.shape[0])
    copy.wait()


def gathered_plan(
    hidden_states, first_gain, second_gain, query_weight, key_weight, value_weight, out_weight, conv_kernel
):
    frames, _, cols, channels = hidden_states.shape
    rows, blocks = lax.axis_size("space"), lax.axis_size("tm")
    own = hidden_states.reshape(frames * cols, channels)
    gains = (first_gain.reshape(1, channels), second_gain.reshape(1, channels))
    by_row = {row: exchange(own, "space", row) for row in range(rows - 1, 0, -1)}
    first = exchange(own, "tm", 1)
    onward = {row: exchange(piece, "tm", 1) for row, piece in by_row.items() if row >= rows // 2}
    for row in range(1, rows // 2):
        onward[row] = exchange(own, ("space", "tm"), row * blocks + 1)
    staged = (query_weight, key_weight, value_weight, out_weight, own, *gains, conv_kernel)
    *weights, own_staged, first_gain, second_gain, first_tap = stage(
        staged, [array.shape[0] for array in staged[:-1]] + [1], by_row[rows // 2]
    )
    near = [own_staged, first]
    for row in range(1, rows // 2):
        near += [by_row[row], onward[row]]
    far = [piece for row in range(rows // 2, rows) for piece in (by_row[row], onward[row])]
    near_mine = pack(near_kernel, near, "near", (first_gain, second_gain))
    near_other = exchange(near_mine, "chan", 1)
    far_mine = pack(pack_kernel, far, "far")
    far_other = exchange(far_mine, "chan", 1)
    in_channels, out_channels = conv_kernel.shape[3:]
    tokens = blocks * frames * rows * cols
    in_vmem = pl.BlockSpec(memory_space=pltpu.VMEM)
    *begun, second_tap = pl.pallas_call(
        functools.partial(mine_kernel, layout=(frames, cols, rows, blocks)),
        out_shape=(jax.ShapeDtypeStruct((tokens, D), jnp.float32),) * 3
        + (jax.ShapeDtypeStruct((1, *conv_kernel.shape[1:]), conv_kernel.dtype),),
        in_specs=[in_vmem] * 5 + [pl.BlockSpec(memory_space=pltpu.HBM)],
        out_specs=(in_vmem,) * 4,
        scratch_shapes=[pltpu.VMEM((tokens, channels), jnp.bfloat16), pltpu.SemaphoreType.DMA],
        compiler_params=pltpu.CompilerParams(vmem_limit_bytes=8 * 1024 * 1024),
        name="mine",
    )(near_mine, far_mine, *weights[:3], in_hbm(conv_kernel))
    attended, activated, send, last_tap = pl.pallas_call(
        main_kernel,
        out_shape=(
            jax.ShapeDtypeStruct((frames, 1, cols, channels), jnp.bfloat16),
            jax.ShapeDtypeStruct((3, blocks * frames + 2, cols, in_channels), jnp.bfloat16),
            jax.ShapeDtypeStruct((frames * cols, out_channels), jnp.bfloat16),
            jax.ShapeDtypeStruct((1, *conv_kernel.shape[1:]), conv_kernel.dtype),
        ),
        in_specs=[in_vmem] * 13 + [pl.BlockSpec(memory_space=pltpu.HBM)],
        out_specs=(in_vmem,) * 4,
        scratch_shapes=[pltpu.VMEM((tokens, channels), jnp.bfloat16)]
        + [pltpu.VMEM((tokens, D), jnp.bfloat16)] * 4
        + [pltpu.VMEM((blocks * frames, rows, cols, in_channels), jnp.float32), pltpu.SemaphoreType.DMA],
        compiler_params=pltpu.CompilerParams(vmem_limit_bytes=24 * 1024 * 1024),
        name="block",
    )(near_mine, far_mine, near_other, far_other, *weights[:3], *begun, weights[3], first_tap, second_tap, in_hbm(conv_kernel))
    received = exchange(send, "tm", 1)
    attended, keep = pl.pallas_call(
        own_kernel,
        out_shape=(
            jax.ShapeDtypeStruct(attended.shape, attended.dtype),
            jax.ShapeDtypeStruct((frames * cols, out_channels), jnp.float32),
        ),
        in_specs=[in_vmem] * 5,
        out_specs=(pl.BlockSpec(memory_space=pl.ANY), in_vmem),
        scratch_shapes=[pltpu.SemaphoreType.DMA],
        compiler_params=pltpu.CompilerParams(vmem_limit_bytes=4 * 1024 * 1024),
        name="own",
    )(activated, first_tap, second_tap, last_tap, attended)
    total = keep + received.astype(jnp.float32)
    return attended, total.astype(jnp.bfloat16).reshape(frames, 1, cols, out_channels)


def power_of_two(count):
    return count & (count - 1) == 0


def on_device(hidden_states, *others):
    frames, rows, cols, channels = hidden_states.shape
    spaces, blocks = lax.axis_size("space"), lax.axis_size("tm")
    tokens = frames * blocks * spaces * rows * cols
    fits = tokens * D <= 2 ** 20 and rows == 1 and lax.axis_size("chan") == 2 and blocks == 2
    if fits and power_of_two(spaces):
        return gathered_plan(hidden_states, *others)
    return split_plan(hidden_states, *others)


def solution(mesh):
    placed = (
        P(("groups", "tm"), "space", None, "chan"),
        P("chan"),
        P("chan"),
        P(),
        P(),
        P(),
        P(),
        P(None, None, None, "tm", "chan"),
    )
    return jax.shard_map(
        on_device,
        mesh=mesh,
        in_specs=placed,
        out_specs=(
            P(("groups", "tm"), "space", None, "chan"),
            P(("groups", "tm"), "space", None, "chan"),
        ),
        check_vma=False,
    )
```

```python
import functools

import jax
import jax.numpy as jnp
from jax import lax
from jax.experimental import pallas as pl
from jax.experimental.pallas import tpu as pltpu
from jax.sharding import PartitionSpec as P

D = 512
NGROUP = 32


EPSILON = 1e-06


def shifted_2(x, axis, by):
    peers = lax.axis_size(axis)
    pairs = [(i, i + by) for i in range(peers) if 0 <= i + by < peers]
    return lax.ppermute(x, axis, pairs)


def padded_2(cells, sides, width):
    for axis, dim in sides:
        count = lax.axis_size(axis)
        ends = count - 1
        head = lax.slice_in_dim(cells, 0, width, axis=dim)
        tail = lax.slice_in_dim(cells, cells.shape[dim] - width, cells.shape[dim], axis=dim)
        cells = jnp.concatenate(
            [
                lax.ppermute(tail, axis, [(i, (i + 1) % count) for i in range(ends)]),
                cells,
                lax.ppermute(head, axis, [((i + 1) % count, i) for i in range(ends)]),
            ],
            axis=dim,
        )
    return cells


def normalize(source, gain_vector):
    channels = source.shape[3]
    group_width = D // NGROUP
    grouped = source.reshape(-1, channels // group_width, group_width)
    population = grouped.shape[0] * group_width * lax.axis_size("space") * lax.axis_size("tm")
    group_sums, group_squares = lax.psum(
        (jnp.sum(grouped, axis=(0, 2)), jnp.sum(grouped * grouped, axis=(0, 2))), ("space", "tm")
    )
    centre = group_sums / population
    spread = jnp.maximum(group_squares / population - centre * centre, 0.0)
    shifted = grouped - centre[None, :, None]
    scaled = shifted * lax.rsqrt(spread + EPSILON)[None, :, None]
    return scaled.reshape(source.shape) * gain_vector


def attend(normed, query_weight, key_weight, value_weight, out_weight):
    frame_count, row_count, col_count, channels = normed.shape
    token_count = frame_count * row_count * col_count
    tokens = normed.reshape(token_count, channels)
    halves = lax.all_to_all(tokens, "chan", split_axis=0, concat_axis=1, tiled=True)
    half_rows = halves.shape[0]
    queries = jnp.dot(halves, query_weight, preferred_element_type=jnp.float32).astype(jnp.bfloat16)
    keyed = jnp.dot(halves, key_weight, preferred_element_type=jnp.float32).astype(jnp.bfloat16)
    valued = jnp.dot(halves, value_weight, preferred_element_type=jnp.float32).astype(jnp.bfloat16)
    score_scale = D ** (-0.5)
    running_max = jnp.full((half_rows,), -1e30, jnp.float32)
    key_piece = lax.all_gather(keyed, "space", axis=0, tiled=True)
    value_piece = lax.all_gather(valued, "space", axis=0, tiled=True)
    scores = jnp.dot(queries, key_piece.T, preferred_element_type=jnp.float32) * score_scale
    newest_max = jnp.maximum(running_max, jnp.max(scores, axis=1))
    weights = jnp.exp(scores - newest_max[:, None])
    running_sum = jnp.sum(weights, axis=1)
    accumulated = jnp.dot(
        weights.astype(jnp.bfloat16), value_piece, preferred_element_type=jnp.float32
    )
    mixed = (accumulated / running_sum[:, None]).astype(jnp.bfloat16)
    projected = jnp.dot(mixed, out_weight, preferred_element_type=jnp.float32).astype(jnp.bfloat16)
    returned = lax.all_to_all(projected, "chan", split_axis=1, concat_axis=0, tiled=True)
    return returned.reshape(frame_count, row_count, col_count, channels)


def join_channels(activated):
    return lax.all_gather(activated, "chan", axis=3, tiled=True)


def extend(frames_in):
    earlier = shifted_2(frames_in, "tm", 1)
    timed = jnp.concatenate([earlier, frames_in], axis=0)
    rimmed = padded_2(timed, (("space", 1),), 1)
    return jnp.pad(rimmed, ((0, 0), (0, 0), (1, 1), (0, 0)))


def convolve(activated, conv_kernel):
    frame_count, row_count, col_count = (activated.shape[0], activated.shape[1], activated.shape[2])
    padded = extend(join_channels(activated))
    out_width = conv_kernel.shape[4]
    initial = jnp.zeros((frame_count * row_count * col_count, out_width), jnp.float32)
    running_total = initial
    piece = lax.all_gather(conv_kernel, "tm", axis=3, tiled=True)
    for time_tap in range(3):
        for row_tap in range(3):
            for col_tap in range(3):
                window = padded[
                    time_tap : time_tap + frame_count,
                    row_tap : row_tap + row_count,
                    col_tap : col_tap + col_count,
                ]
                window = window.reshape(frame_count * row_count * col_count, piece.shape[3])
                running_total = running_total + jnp.dot(
                    window, piece[time_tap, row_tap, col_tap], preferred_element_type=jnp.float32
                )
    return running_total.reshape(frame_count, row_count, col_count, out_width).astype(jnp.bfloat16)


def split_plan(
    hidden_states,
    first_gain,
    second_gain,
    query_weight,
    key_weight,
    value_weight,
    out_weight,
    conv_kernel,
):
    source = hidden_states.astype(jnp.float32)
    normed = normalize(source, first_gain).astype(jnp.bfloat16)
    attended = attend(normed, query_weight, key_weight, value_weight, out_weight)
    resid = source + attended.astype(jnp.float32)
    activated = jax.nn.silu(normalize(resid, second_gain)).astype(jnp.bfloat16)
    convolved = convolve(activated, conv_kernel)
    return (attended, convolved)


GAIN_ROWS = 16


def exchange(x, axes, step):
    peers = lax.axis_size(axes)
    return lax.ppermute(x, axes, [(i, i ^ step) for i in range(peers)])


def stage_kernel(
    query_hbm, key_hbm, value_hbm, out_weight_hbm, own_hbm, first_hbm, second_hbm, kernel_hbm, _,
    query_ref, key_ref, value_ref, in_out_ref, own_out_ref, own_ref, first_ref, second_ref, tap_ref, arrived,
):
    channels, in_channels = own_out_ref.shape[1], in_out_ref.shape[1]
    own_half = pl.ds(pl.multiple_of(lax.axis_index("chan") * channels, channels), channels)
    in_half = pl.ds(pl.multiple_of(lax.axis_index("tm") * in_channels, in_channels), in_channels)
    moves = []
    other_half = pl.ds(pl.multiple_of((1 - lax.axis_index("chan")) * channels, channels), channels)
    for source, target in ((query_hbm, query_ref), (key_hbm, key_ref), (value_hbm, value_ref)):
        moves.append((source.at[own_half], target.at[pl.ds(0, channels)]))
        moves.append((source.at[other_half], target.at[pl.ds(channels, channels)]))
    moves += [
        (out_weight_hbm.at[:, in_half], in_out_ref), (out_weight_hbm.at[:, own_half], own_out_ref),
        (own_hbm, own_ref), (first_hbm, first_ref), (second_hbm, second_ref), (kernel_hbm.at[pl.ds(0, tap_ref.shape[0])], tap_ref),
    ]
    copies = [pltpu.make_async_copy(*move, arrived.at[place]) for place, move in enumerate(moves)]
    for copy in copies:
        copy.start()
    for copy in copies:
        copy.wait()


def stage(arrays, after):
    query_weight, _, _, out_weight, own, first_gain, second_gain, conv_kernel = arrays
    in_channels = conv_kernel.shape[3]
    shapes = [query_weight.shape] * 3 + [(out_weight.shape[0], in_channels), (out_weight.shape[0], own.shape[1])]
    shapes = [jax.ShapeDtypeStruct(shape, own.dtype) for shape in shapes + [own.shape, (conv_kernel.shape[0] - 1, *conv_kernel.shape[1:])]]
    gains = [jax.ShapeDtypeStruct(gain.shape, gain.dtype) for gain in (first_gain, second_gain)]
    shapes = shapes[:-1] + gains + shapes[-1:]
    return pl.pallas_call(
        stage_kernel,
        out_shape=tuple(shapes),
        in_specs=[pl.BlockSpec(memory_space=pltpu.HBM)] * len(arrays) + [pl.BlockSpec(memory_space=pl.ANY)],
        out_specs=tuple(pl.BlockSpec(memory_space=pltpu.VMEM) for _ in shapes),
        scratch_shapes=[pltpu.SemaphoreType.DMA((12,))],
        compiler_params=pltpu.CompilerParams(vmem_limit_bytes=1 << 20),
        name="stage",
    )(*(in_hbm(array) for array in arrays), after)


def pack_kernel(*refs):
    end = 0
    for piece_ref in refs[:-1]:
        start, end = end, end + piece_ref.shape[0]
        refs[-1][start:end, :] = piece_ref[...]


def near_kernel(first_ref, second_ref, *refs):
    pack_kernel(*refs)
    parts = split_parts(first_ref[...]) + split_parts(second_ref[...])
    parts = [part.astype(jnp.float32) for part in parts]
    parts.append(jnp.zeros((GAIN_ROWS - len(parts), first_ref.shape[1]), jnp.float32))
    end = refs[-1].shape[0]
    refs[-1][end - GAIN_ROWS : end, :] = jnp.concatenate(parts, axis=0).astype(jnp.bfloat16)


def pack(kernel, pieces, name, gains=()):
    size = sum(piece.shape[0] for piece in pieces) + (GAIN_ROWS if gains else 0)
    return pl.pallas_call(
        kernel,
        out_shape=jax.ShapeDtypeStruct((size, pieces[0].shape[1]), pieces[0].dtype),
        compiler_params=pltpu.CompilerParams(vmem_limit_bytes=2 * 1024 * 1024),
        name=name,
    )(*gains, *pieces)


def in_hbm(array):
    return pltpu.with_memory_space_constraint(array, pltpu.HBM)


def split_parts(values):
    parts = []
    for _ in range(3):
        rounded = values.astype(jnp.bfloat16)
        parts.append(rounded)
        values = values - rounded.astype(jnp.float32)
    return parts


def group_statistics(rows, count):
    channels = rows[0].shape[1]
    width = D // NGROUP
    left = lax.broadcasted_iota(jnp.int32, (channels, channels), 0) // width
    right = lax.broadcasted_iota(jnp.int32, (channels, channels), 1) // width
    member = jnp.where(left == right, 1.0, 0.0).astype(jnp.bfloat16)
    parts = [part for row in rows for part in split_parts(row)]
    parts += [jnp.zeros((1, channels), jnp.bfloat16)] * (16 - len(parts))
    totals = jnp.dot(jnp.concatenate(parts, axis=0), member, preferred_element_type=jnp.float32)
    means = [
        (totals[at : at + 1] + totals[at + 1 : at + 2] + totals[at + 2 : at + 3]) * (1.0 / count)
        for at in range(0, 3 * len(rows), 3)
    ]
    found = []
    for centre, square in zip(means[::2], means[1::2]):
        spread = jnp.maximum(square - centre * centre, 0.0)
        found.append((centre, lax.rsqrt(spread + EPSILON)))
    return found


def core_chunks(near, far, layout):
    own_frames, cols, rows, blocks = layout
    size = own_frames * cols
    places = [(ref, at) for ref in (near, far) for at in range(0, ref.shape[0] - size + 1, size)]
    chunks = []
    for index in range(blocks):
        for frame in range(own_frames):
            for row in range(rows):
                ref, at = places[row * blocks + index]
                chunks.append((ref, slice(at + frame * cols, at + (frame + 1) * cols)))
    return chunks


def core_gain(near, which):
    end = near.shape[0]
    parts = near[end - GAIN_ROWS : end, :].astype(jnp.float32)
    at = 3 * which
    return parts[at : at + 1] + parts[at + 1 : at + 2] + parts[at + 2 : at + 3]


def add_chunk(totals, values):
    parts = values.reshape(values.shape[0] // 8, 8, values.shape[1])
    found = [jnp.sum(parts, axis=0), jnp.sum(parts * parts, axis=0)]
    return found if totals is None else [total + part for total, part in zip(totals, found)]


def chunk_statistics(totals, count):
    ((centre, scale),) = group_statistics([jnp.sum(total, axis=0, keepdims=True) for total in totals], count)
    return centre, scale


def norm_chunks(chunks, gain, normed):
    totals = None
    for ref, at in chunks:
        totals = add_chunk(totals, ref[at, :].astype(jnp.float32))
    centre, scale = chunk_statistics(totals, normed.shape[0] * (D // NGROUP))
    scale = scale * gain
    end = 0
    for ref, at in chunks:
        start, end = end, end + at.stop - at.start
        normed[start:end, :] = ((ref[at, :].astype(jnp.float32) - centre) * scale).astype(jnp.bfloat16)


def mine_kernel(
    near_ref, far_ref, query_ref, key_ref, value_ref, kernel_hbm,
    begun_query, begun_key, begun_value, last_tap, normed, arrived, *, layout,
):
    copy = pltpu.make_async_copy(kernel_hbm.at[pl.ds(kernel_hbm.shape[0] - 1, 1)], last_tap, arrived)
    copy.start()
    norm_chunks(core_chunks(near_ref, far_ref, layout), core_gain(near_ref, 0), normed)
    channels = normed.shape[1]
    for weight_ref, target in zip((query_ref, key_ref, value_ref), (begun_query, begun_key, begun_value)):
        target[...] = jnp.dot(normed[...], weight_ref[:channels, :], preferred_element_type=jnp.float32)
    copy.wait()


def main_kernel(
    near_ref, far_ref, other_near_ref, other_far_ref, query_ref, key_ref, value_ref, begun_query, begun_key, begun_value,
    in_out_ref, own_out_ref, early_taps, last_tap,
    attended_ref, activated, send_ref,
    normed, queries, keyed, valued, mixed, resid, projected,
):
    own_frames, _, cols, channels = attended_ref.shape
    frames, rows = resid.shape[:2]
    tokens = frames * rows * cols
    frame_tokens = rows * cols
    space = lax.axis_index("space")
    block = lax.axis_index("tm")
    half = lax.axis_index("chan")
    width = D // NGROUP
    count = tokens * width

    blocks = frames // own_frames

    layout = (own_frames, cols, rows, blocks)
    mine, other = core_chunks(near_ref, far_ref, layout), core_chunks(other_near_ref, other_far_ref, layout)
    norm_chunks(other, core_gain(other_near_ref, 0), normed)
    for weight_ref, begun_ref, target in zip(
        (query_ref, key_ref, value_ref), (begun_query, begun_key, begun_value), (queries, keyed, valued)
    ):
        term = jnp.dot(normed[...], weight_ref[channels:, :], preferred_element_type=jnp.float32)
        target[...] = (begun_ref[...] + term).astype(jnp.bfloat16)

    in_channels = early_taps.shape[3]
    mine_in = block == half
    spans = [slice(frame * frame_tokens, (frame + 1) * frame_tokens) for frame in range(frames)]
    scores = [
        lax.dot_general(queries[at, :], keyed[at, :], (((1,), (1,)), ((), ())), preferred_element_type=jnp.float32)
        for at in spans
    ]
    for at, score in zip(spans, scores):
        peak = jnp.max(score, axis=1, keepdims=True)
        weights = jnp.exp((score - peak) * (D ** (-0.5)))
        mass = jnp.sum(weights, axis=1, keepdims=True)
        blend = jnp.dot(weights.astype(jnp.bfloat16), valued[at, :], preferred_element_type=jnp.float32)
        mixed[at, :] = (blend * (1.0 / mass)).astype(jnp.bfloat16)
    projected[...] = jnp.dot(mixed[...], in_out_ref[...], preferred_element_type=jnp.float32).astype(jnp.bfloat16)
    totals = None
    for chunk, ((ref, at), (other_ref, _)) in enumerate(zip(mine, other)):
        source = jnp.where(mine_in, ref[at, :], other_ref[at, :]).astype(jnp.float32)
        total = source + projected[chunk * cols : (chunk + 1) * cols, :].astype(jnp.float32)
        resid[chunk // rows, chunk % rows] = total
        totals = add_chunk(totals, total)
    own_mixed = jnp.concatenate([mixed[at.start : at.start + cols, :] for at in spans[:own_frames]], axis=0)
    attended_ref[...] = jnp.dot(
        own_mixed, own_out_ref[...], preferred_element_type=jnp.float32
    ).astype(jnp.bfloat16).reshape(own_frames, 1, cols, channels)

    centre, scale = chunk_statistics(totals, count)
    scale = 0.5 * scale * jnp.where(mine_in, core_gain(near_ref, 1), core_gain(other_near_ref, 1))
    activated[:, 0:2] = jnp.zeros((3, 2, cols, in_channels), jnp.bfloat16)
    for tap in range(3):
        row = space + (tap - 1)
        inside = jnp.logical_and(row >= 0, row < rows)
        place = jnp.where(inside, space ^ row, 0)
        row_scale = jnp.where(inside, scale, 0.0)
        for frame in range(frames):
            relative = ((frame // own_frames) ^ block) * own_frames + frame % own_frames
            halved = (resid[relative, place] - centre) * row_scale
            activated[tap, frame + 2] = (halved + halved * jnp.tanh(halved)).astype(jnp.bfloat16)

    send_ref[...] = partial_conv(activated, early_taps, last_tap, 1 - block, own_frames).astype(jnp.bfloat16)


def partial_conv(activated, early_taps, last_tap, block, frames):
    cols, in_channels = activated.shape[2:]
    tokens = frames * cols
    taps = [ref.at[tap] for ref in (early_taps, last_tap) for tap in range(ref.shape[0])]
    columns = []
    for col_tap in range(3):
        total = None
        for time_tap in range(3):
            for row_tap in range(3):
                window = activated[row_tap, pl.ds(block * frames + time_tap, frames)].reshape(tokens, in_channels)
                term = jnp.dot(window, taps[time_tap][row_tap, col_tap], preferred_element_type=jnp.float32)
                total = term if total is None else total + term
        columns.append(total)
    place = lax.broadcasted_iota(jnp.int32, columns[0].shape, 0) % cols
    left = jnp.where(place == 0, 0.0, pltpu.roll(columns[0], 1, 0))
    right = jnp.where(place == cols - 1, 0.0, pltpu.roll(columns[2], tokens - 1, 0))
    return columns[1] + left + right


def own_kernel(activated, early_taps, last_tap, attended_ref, attended_hbm, keep_ref, sent):
    copy = pltpu.make_async_copy(attended_ref, attended_hbm, sent)
    copy.start()
    keep_ref[...] = partial_conv(activated, early_taps, last_tap, lax.axis_index("tm"), attended_ref.shape[0])
    copy.wait()


def gathered_plan(
    hidden_states, first_gain, second_gain, query_weight, key_weight, value_weight, out_weight, conv_kernel
):
    frames, _, cols, channels = hidden_states.shape
    rows, blocks = lax.axis_size("space"), lax.axis_size("tm")
    own = hidden_states.reshape(frames * cols, channels)
    gains = (first_gain.reshape(1, channels), second_gain.reshape(1, channels))
    by_row = {row: exchange(own, "space", row) for row in range(rows - 1, 0, -1)}
    first = exchange(own, "tm", 1)
    onward = {row: exchange(piece, "tm", 1) for row, piece in by_row.items() if row >= rows // 2}
    for row in range(1, rows // 2):
        onward[row] = exchange(own, ("space", "tm"), row * blocks + 1)
    staged = (query_weight, key_weight, value_weight, out_weight, own, *gains, conv_kernel)
    *weights, in_out, own_out, own_staged, first_gain, second_gain, early_taps = stage(staged, by_row[rows // 2])
    near = [own_staged, first]
    for row in range(1, rows // 2):
        near += [by_row[row], onward[row]]
    far = [piece for row in range(rows // 2, rows) for piece in (by_row[row], onward[row])]
    near_mine = pack(near_kernel, near, "near", (first_gain, second_gain))
    near_other = exchange(near_mine, "chan", 1)
    far_mine = pack(pack_kernel, far, "far")
    far_other = exchange(far_mine, "chan", 1)
    in_channels, out_channels = conv_kernel.shape[3:]
    tokens = blocks * frames * rows * cols
    in_vmem = pl.BlockSpec(memory_space=pltpu.VMEM)
    *begun, last_tap = pl.pallas_call(
        functools.partial(mine_kernel, layout=(frames, cols, rows, blocks)),
        out_shape=(jax.ShapeDtypeStruct((tokens, D), jnp.float32),) * 3
        + (jax.ShapeDtypeStruct((1, *conv_kernel.shape[1:]), conv_kernel.dtype),),
        in_specs=[in_vmem] * 5 + [pl.BlockSpec(memory_space=pltpu.HBM)],
        out_specs=(in_vmem,) * 4,
        scratch_shapes=[pltpu.VMEM((tokens, channels), jnp.bfloat16), pltpu.SemaphoreType.DMA],
        compiler_params=pltpu.CompilerParams(vmem_limit_bytes=8 * 1024 * 1024),
        name="mine",
    )(near_mine, far_mine, *weights, in_hbm(conv_kernel))
    attended, activated, send = pl.pallas_call(
        main_kernel,
        out_shape=(
            jax.ShapeDtypeStruct((frames, 1, cols, channels), jnp.bfloat16),
            jax.ShapeDtypeStruct((3, blocks * frames + 2, cols, in_channels), jnp.bfloat16),
            jax.ShapeDtypeStruct((frames * cols, out_channels), jnp.bfloat16),
        ),
        in_specs=[in_vmem] * 14,
        out_specs=(in_vmem,) * 3,
        scratch_shapes=[pltpu.VMEM((tokens, channels), jnp.bfloat16)]
        + [pltpu.VMEM((tokens, D), jnp.bfloat16)] * 4
        + [pltpu.VMEM((blocks * frames, rows, cols, in_channels), jnp.float32)]
        + [pltpu.VMEM((tokens, in_channels), jnp.bfloat16)],
        compiler_params=pltpu.CompilerParams(vmem_limit_bytes=24 * 1024 * 1024),
        name="block",
    )(near_mine, far_mine, near_other, far_other, *weights, *begun, in_out, own_out, early_taps, last_tap)
    received = exchange(send, "tm", 1)
    attended, keep = pl.pallas_call(
        own_kernel,
        out_shape=(
            jax.ShapeDtypeStruct(attended.shape, attended.dtype),
            jax.ShapeDtypeStruct((frames * cols, out_channels), jnp.float32),
        ),
        in_specs=[in_vmem] * 4,
        out_specs=(pl.BlockSpec(memory_space=pl.ANY), in_vmem),
        scratch_shapes=[pltpu.SemaphoreType.DMA],
        compiler_params=pltpu.CompilerParams(vmem_limit_bytes=4 * 1024 * 1024),
        name="own",
    )(activated, early_taps, last_tap, attended)
    total = keep + received.astype(jnp.float32)
    return attended, total.astype(jnp.bfloat16).reshape(frames, 1, cols, out_channels)


def power_of_two(count):
    return count & (count - 1) == 0


def on_device(hidden_states, *others):
    frames, rows, cols, channels = hidden_states.shape
    spaces, blocks = lax.axis_size("space"), lax.axis_size("tm")
    tokens = frames * blocks * spaces * rows * cols
    fits = tokens * D <= 2 ** 20 and rows == 1 and lax.axis_size("chan") == 2 and blocks == 2
    if fits and power_of_two(spaces):
        return gathered_plan(hidden_states, *others)
    return split_plan(hidden_states, *others)


def solution(mesh):
    placed = (
        P(("groups", "tm"), "space", None, "chan"),
        P("chan"),
        P("chan"),
        P(),
        P(),
        P(),
        P(),
        P(None, None, None, "tm", "chan"),
    )
    return jax.shard_map(
        on_device,
        mesh=mesh,
        in_specs=placed,
        out_specs=(
            P(("groups", "tm"), "space", None, "chan"),
            P(("groups", "tm"), "space", None, "chan"),
        ),
        check_vma=False,
    )
```

```python
import functools

import jax
import jax.numpy as jnp
from jax import lax
from jax.experimental import pallas as pl
from jax.experimental.pallas import tpu as pltpu
from jax.sharding import PartitionSpec as P

D = 512
NGROUP = 32


EPSILON = 1e-06


def shifted_2(x, axis, by):
    peers = lax.axis_size(axis)
    pairs = [(i, i + by) for i in range(peers) if 0 <= i + by < peers]
    return lax.ppermute(x, axis, pairs)


def padded_2(cells, sides, width):
    for axis, dim in sides:
        count = lax.axis_size(axis)
        ends = count - 1
        head = lax.slice_in_dim(cells, 0, width, axis=dim)
        tail = lax.slice_in_dim(cells, cells.shape[dim] - width, cells.shape[dim], axis=dim)
        cells = jnp.concatenate(
            [
                lax.ppermute(tail, axis, [(i, (i + 1) % count) for i in range(ends)]),
                cells,
                lax.ppermute(head, axis, [((i + 1) % count, i) for i in range(ends)]),
            ],
            axis=dim,
        )
    return cells


def normalize(source, gain_vector):
    channels = source.shape[3]
    group_width = D // NGROUP
    grouped = source.reshape(-1, channels // group_width, group_width)
    population = grouped.shape[0] * group_width * lax.axis_size("space") * lax.axis_size("tm")
    group_sums, group_squares = lax.psum(
        (jnp.sum(grouped, axis=(0, 2)), jnp.sum(grouped * grouped, axis=(0, 2))), ("space", "tm")
    )
    centre = group_sums / population
    spread = jnp.maximum(group_squares / population - centre * centre, 0.0)
    shifted = grouped - centre[None, :, None]
    scaled = shifted * lax.rsqrt(spread + EPSILON)[None, :, None]
    return scaled.reshape(source.shape) * gain_vector


def attend(normed, query_weight, key_weight, value_weight, out_weight):
    frame_count, row_count, col_count, channels = normed.shape
    token_count = frame_count * row_count * col_count
    tokens = normed.reshape(token_count, channels)
    halves = lax.all_to_all(tokens, "chan", split_axis=0, concat_axis=1, tiled=True)
    half_rows = halves.shape[0]
    queries = jnp.dot(halves, query_weight, preferred_element_type=jnp.float32).astype(jnp.bfloat16)
    keyed = jnp.dot(halves, key_weight, preferred_element_type=jnp.float32).astype(jnp.bfloat16)
    valued = jnp.dot(halves, value_weight, preferred_element_type=jnp.float32).astype(jnp.bfloat16)
    score_scale = D ** (-0.5)
    running_max = jnp.full((half_rows,), -1e30, jnp.float32)
    key_piece = lax.all_gather(keyed, "space", axis=0, tiled=True)
    value_piece = lax.all_gather(valued, "space", axis=0, tiled=True)
    scores = jnp.dot(queries, key_piece.T, preferred_element_type=jnp.float32) * score_scale
    newest_max = jnp.maximum(running_max, jnp.max(scores, axis=1))
    weights = jnp.exp(scores - newest_max[:, None])
    running_sum = jnp.sum(weights, axis=1)
    accumulated = jnp.dot(
        weights.astype(jnp.bfloat16), value_piece, preferred_element_type=jnp.float32
    )
    mixed = (accumulated / running_sum[:, None]).astype(jnp.bfloat16)
    projected = jnp.dot(mixed, out_weight, preferred_element_type=jnp.float32).astype(jnp.bfloat16)
    returned = lax.all_to_all(projected, "chan", split_axis=1, concat_axis=0, tiled=True)
    return returned.reshape(frame_count, row_count, col_count, channels)


def join_channels(activated):
    return lax.all_gather(activated, "chan", axis=3, tiled=True)


def extend(frames_in):
    earlier = shifted_2(frames_in, "tm", 1)
    timed = jnp.concatenate([earlier, frames_in], axis=0)
    rimmed = padded_2(timed, (("space", 1),), 1)
    return jnp.pad(rimmed, ((0, 0), (0, 0), (1, 1), (0, 0)))


def convolve(activated, conv_kernel):
    frame_count, row_count, col_count = (activated.shape[0], activated.shape[1], activated.shape[2])
    padded = extend(join_channels(activated))
    out_width = conv_kernel.shape[4]
    initial = jnp.zeros((frame_count * row_count * col_count, out_width), jnp.float32)
    running_total = initial
    piece = lax.all_gather(conv_kernel, "tm", axis=3, tiled=True)
    for time_tap in range(3):
        for row_tap in range(3):
            for col_tap in range(3):
                window = padded[
                    time_tap : time_tap + frame_count,
                    row_tap : row_tap + row_count,
                    col_tap : col_tap + col_count,
                ]
                window = window.reshape(frame_count * row_count * col_count, piece.shape[3])
                running_total = running_total + jnp.dot(
                    window, piece[time_tap, row_tap, col_tap], preferred_element_type=jnp.float32
                )
    return running_total.reshape(frame_count, row_count, col_count, out_width).astype(jnp.bfloat16)


def split_plan(
    hidden_states,
    first_gain,
    second_gain,
    query_weight,
    key_weight,
    value_weight,
    out_weight,
    conv_kernel,
):
    source = hidden_states.astype(jnp.float32)
    normed = normalize(source, first_gain).astype(jnp.bfloat16)
    attended = attend(normed, query_weight, key_weight, value_weight, out_weight)
    resid = source + attended.astype(jnp.float32)
    activated = jax.nn.silu(normalize(resid, second_gain)).astype(jnp.bfloat16)
    convolved = convolve(activated, conv_kernel)
    return (attended, convolved)


GAIN_ROWS = 16


def exchange(x, axes, step):
    peers = lax.axis_size(axes)
    return lax.ppermute(x, axes, [(i, i ^ step) for i in range(peers)])


def stage_kernel(
    query_hbm, key_hbm, value_hbm, out_weight_hbm, own_hbm, first_hbm, second_hbm, kernel_hbm, _,
    query_ref, key_ref, value_ref, in_out_ref, own_out_ref, own_ref, first_ref, second_ref, tap_ref, arrived,
):
    channels, in_channels = own_out_ref.shape[1], in_out_ref.shape[1]
    own_half = pl.ds(pl.multiple_of(lax.axis_index("chan") * channels, channels), channels)
    in_half = pl.ds(pl.multiple_of(lax.axis_index("tm") * in_channels, in_channels), in_channels)
    moves = []
    other_half = pl.ds(pl.multiple_of((1 - lax.axis_index("chan")) * channels, channels), channels)
    for source, target in ((query_hbm, query_ref), (key_hbm, key_ref), (value_hbm, value_ref)):
        moves.append((source.at[own_half], target.at[pl.ds(0, channels)]))
        moves.append((source.at[other_half], target.at[pl.ds(channels, channels)]))
    moves += [
        (out_weight_hbm.at[:, in_half], in_out_ref), (out_weight_hbm.at[:, own_half], own_out_ref),
        (own_hbm, own_ref), (first_hbm, first_ref), (second_hbm, second_ref), (kernel_hbm.at[pl.ds(0, tap_ref.shape[0])], tap_ref),
    ]
    copies = [pltpu.make_async_copy(*move, arrived.at[place]) for place, move in enumerate(moves)]
    for copy in copies:
        copy.start()
    for copy in copies:
        copy.wait()


def stage(arrays, after):
    query_weight, _, _, out_weight, own, first_gain, second_gain, conv_kernel = arrays
    in_channels = conv_kernel.shape[3]
    shapes = [query_weight.shape] * 3 + [(out_weight.shape[0], in_channels), (out_weight.shape[0], own.shape[1])]
    shapes = [jax.ShapeDtypeStruct(shape, own.dtype) for shape in shapes + [own.shape, (conv_kernel.shape[0] - 1, *conv_kernel.shape[1:])]]
    gains = [jax.ShapeDtypeStruct(gain.shape, gain.dtype) for gain in (first_gain, second_gain)]
    shapes = shapes[:-1] + gains + shapes[-1:]
    return pl.pallas_call(
        stage_kernel,
        out_shape=tuple(shapes),
        in_specs=[pl.BlockSpec(memory_space=pltpu.HBM)] * len(arrays) + [pl.BlockSpec(memory_space=pl.ANY)],
        out_specs=tuple(pl.BlockSpec(memory_space=pltpu.VMEM) for _ in shapes),
        scratch_shapes=[pltpu.SemaphoreType.DMA((12,))],
        compiler_params=pltpu.CompilerParams(vmem_limit_bytes=1 << 20),
        name="stage",
    )(*(in_hbm(array) for array in arrays), after)


def pack_kernel(*refs):
    end = 0
    for piece_ref in refs[:-1]:
        start, end = end, end + piece_ref.shape[0]
        refs[-1][start:end, :] = piece_ref[...]


def near_kernel(first_ref, second_ref, *refs):
    pack_kernel(*refs)
    parts = split_parts(first_ref[...]) + split_parts(second_ref[...])
    parts = [part.astype(jnp.float32) for part in parts]
    parts.append(jnp.zeros((GAIN_ROWS - len(parts), first_ref.shape[1]), jnp.float32))
    end = refs[-1].shape[0]
    refs[-1][end - GAIN_ROWS : end, :] = jnp.concatenate(parts, axis=0).astype(jnp.bfloat16)


def pack(kernel, pieces, name, gains=()):
    size = sum(piece.shape[0] for piece in pieces) + (GAIN_ROWS if gains else 0)
    return pl.pallas_call(
        kernel,
        out_shape=jax.ShapeDtypeStruct((size, pieces[0].shape[1]), pieces[0].dtype),
        compiler_params=pltpu.CompilerParams(vmem_limit_bytes=2 * 1024 * 1024),
        name=name,
    )(*gains, *pieces)


def in_hbm(array):
    return pltpu.with_memory_space_constraint(array, pltpu.HBM)


def split_parts(values):
    parts = []
    for _ in range(3):
        rounded = values.astype(jnp.bfloat16)
        parts.append(rounded)
        values = values - rounded.astype(jnp.float32)
    return parts


def group_statistics(rows, count):
    channels = rows[0].shape[1]
    width = D // NGROUP
    left = lax.broadcasted_iota(jnp.int32, (channels, channels), 0) // width
    right = lax.broadcasted_iota(jnp.int32, (channels, channels), 1) // width
    member = jnp.where(left == right, 1.0, 0.0).astype(jnp.bfloat16)
    parts = [part for row in rows for part in split_parts(row)]
    parts += [jnp.zeros((1, channels), jnp.bfloat16)] * (16 - len(parts))
    totals = jnp.dot(jnp.concatenate(parts, axis=0), member, preferred_element_type=jnp.float32)
    means = [
        (totals[at : at + 1] + totals[at + 1 : at + 2] + totals[at + 2 : at + 3]) * (1.0 / count)
        for at in range(0, 3 * len(rows), 3)
    ]
    found = []
    for centre, square in zip(means[::2], means[1::2]):
        spread = jnp.maximum(square - centre * centre, 0.0)
        found.append((centre, lax.rsqrt(spread + EPSILON)))
    return found


def core_chunks(near, far, layout):
    own_frames, cols, rows, blocks = layout
    size = own_frames * cols
    places = [(ref, at) for ref in (near, far) for at in range(0, ref.shape[0] - size + 1, size)]
    chunks = []
    for index in range(blocks):
        for frame in range(own_frames):
            for row in range(rows):
                ref, at = places[row * blocks + index]
                chunks.append((ref, slice(at + frame * cols, at + (frame + 1) * cols)))
    return chunks


def core_gain(near, which):
    end = near.shape[0]
    parts = near[end - GAIN_ROWS : end, :].astype(jnp.float32)
    at = 3 * which
    return parts[at : at + 1] + parts[at + 1 : at + 2] + parts[at + 2 : at + 3]


def add_chunk(totals, values):
    parts = values.reshape(values.shape[0] // 8, 8, values.shape[1])
    found = [jnp.sum(parts, axis=0), jnp.sum(parts * parts, axis=0)]
    return found if totals is None else [total + part for total, part in zip(totals, found)]


def chunk_statistics(totals, count):
    ((centre, scale),) = group_statistics([jnp.sum(total, axis=0, keepdims=True) for total in totals], count)
    return centre, scale


def norm_chunks(chunks, gain, normed):
    totals = None
    for ref, at in chunks:
        totals = add_chunk(totals, ref[at, :].astype(jnp.float32))
    centre, scale = chunk_statistics(totals, normed.shape[0] * (D // NGROUP))
    scale = scale * gain
    end = 0
    for ref, at in chunks:
        start, end = end, end + at.stop - at.start
        normed[start:end, :] = ((ref[at, :].astype(jnp.float32) - centre) * scale).astype(jnp.bfloat16)


def mine_kernel(
    near_ref, far_ref, query_ref, key_ref, value_ref, kernel_hbm,
    begun_query, begun_key, begun_value, last_tap, normed, arrived, *, layout,
):
    copy = pltpu.make_async_copy(kernel_hbm.at[pl.ds(kernel_hbm.shape[0] - 1, 1)], last_tap, arrived)
    copy.start()
    norm_chunks(core_chunks(near_ref, far_ref, layout), core_gain(near_ref, 0), normed)
    channels = normed.shape[1]
    for weight_ref, target in zip((query_ref, key_ref, value_ref), (begun_query, begun_key, begun_value)):
        target[...] = jnp.dot(normed[...], weight_ref[:channels, :], preferred_element_type=jnp.float32)
    copy.wait()


def main_kernel(
    near_ref, far_ref, other_near_ref, other_far_ref, query_ref, key_ref, value_ref, begun_query, begun_key, begun_value,
    in_out_ref, early_taps, last_tap,
    own_mixed, activated, send_ref,
    normed, queries, keyed, valued, mixed, resid, projected,
):
    frames, rows, cols, channels = resid.shape
    own_frames = own_mixed.shape[0] // cols
    tokens = frames * rows * cols
    frame_tokens = rows * cols
    space = lax.axis_index("space")
    block = lax.axis_index("tm")
    half = lax.axis_index("chan")
    width = D // NGROUP
    count = tokens * width

    blocks = frames // own_frames

    layout = (own_frames, cols, rows, blocks)
    mine, other = core_chunks(near_ref, far_ref, layout), core_chunks(other_near_ref, other_far_ref, layout)
    norm_chunks(other, core_gain(other_near_ref, 0), normed)
    in_channels = early_taps.shape[3]
    mine_in = block == half
    spans = [slice(frame * frame_tokens, (frame + 1) * frame_tokens) for frame in range(frames)]
    for weight_ref, begun_ref, target in ((query_ref, begun_query, queries), (key_ref, begun_key, keyed)):
        term = jnp.dot(normed[...], weight_ref[channels:, :], preferred_element_type=jnp.float32)
        target[...] = (begun_ref[...] + term).astype(jnp.bfloat16)
    scores = [
        lax.dot_general(queries[at, :], keyed[at, :], (((1,), (1,)), ((), ())), preferred_element_type=jnp.float32)
        for at in spans
    ]
    for weight_ref, begun_ref, target in ((value_ref, begun_value, valued),):
        term = jnp.dot(normed[...], weight_ref[channels:, :], preferred_element_type=jnp.float32)
        target[...] = (begun_ref[...] + term).astype(jnp.bfloat16)
    for at, score in zip(spans, scores):
        peak = jnp.max(score, axis=1, keepdims=True)
        weights = jnp.exp((score - peak) * (D ** (-0.5)))
        mass = jnp.sum(weights, axis=1, keepdims=True)
        blend = jnp.dot(weights.astype(jnp.bfloat16), valued[at, :], preferred_element_type=jnp.float32)
        mixed[at, :] = (blend * (1.0 / mass)).astype(jnp.bfloat16)
    projected[...] = jnp.dot(mixed[...], in_out_ref[...], preferred_element_type=jnp.float32).astype(jnp.bfloat16)
    totals = None
    for chunk, ((ref, at), (other_ref, _)) in enumerate(zip(mine, other)):
        source = jnp.where(mine_in, ref[at, :], other_ref[at, :]).astype(jnp.float32)
        total = source + projected[chunk * cols : (chunk + 1) * cols, :].astype(jnp.float32)
        resid[chunk // rows, chunk % rows] = total
        totals = add_chunk(totals, total)
    size = own_mixed.shape[0] // own_frames
    for frame, at in enumerate(spans[:own_frames]):
        own_mixed[frame * size : (frame + 1) * size, :] = mixed[at.start : at.start + size, :]

    centre, scale = chunk_statistics(totals, count)
    scale = 0.5 * scale * jnp.where(mine_in, core_gain(near_ref, 1), core_gain(other_near_ref, 1))
    activated[:, 0:2] = jnp.zeros((3, 2, cols, in_channels), jnp.bfloat16)
    for tap in range(3):
        row = space + (tap - 1)
        inside = jnp.logical_and(row >= 0, row < rows)
        place = jnp.where(inside, space ^ row, 0)
        row_scale = jnp.where(inside, scale, 0.0)
        for frame in range(frames):
            relative = ((frame // own_frames) ^ block) * own_frames + frame % own_frames
            halved = (resid[relative, place] - centre) * row_scale
            activated[tap, frame + 2] = (halved + halved * jnp.tanh(halved)).astype(jnp.bfloat16)

    send_ref[...] = partial_conv(activated, early_taps, last_tap, 1 - block, own_frames).astype(jnp.bfloat16)


def partial_conv(activated, early_taps, last_tap, block, frames):
    cols, in_channels = activated.shape[2:]
    tokens = frames * cols
    taps = [ref.at[tap] for ref in (early_taps, last_tap) for tap in range(ref.shape[0])]
    columns = []
    for col_tap in range(3):
        total = None
        for time_tap in range(3):
            start = block * frames + time_tap
            windows = [activated[row_tap, pl.ds(start, frames)].reshape(tokens, in_channels) for row_tap in range(3)]
            term = jnp.dot(
                jnp.concatenate(windows, axis=1),
                taps[time_tap][:, col_tap].reshape(3 * in_channels, -1),
                preferred_element_type=jnp.float32,
            )
            total = term if total is None else total + term
        columns.append(total)
    place = lax.broadcasted_iota(jnp.int32, columns[0].shape, 0) % cols
    left = jnp.where(place == 0, 0.0, pltpu.roll(columns[0], 1, 0))
    right = jnp.where(place == cols - 1, 0.0, pltpu.roll(columns[2], tokens - 1, 0))
    return columns[1] + left + right


def own_kernel(activated, early_taps, last_tap, own_mixed, own_out_ref, attended_hbm, keep_ref, attended_ref, sent):
    attended_ref[...] = jnp.dot(
        own_mixed[...], own_out_ref[...], preferred_element_type=jnp.float32
    ).astype(jnp.bfloat16).reshape(attended_ref.shape)
    copy = pltpu.make_async_copy(attended_ref, attended_hbm, sent)
    copy.start()
    keep_ref[...] = partial_conv(activated, early_taps, last_tap, lax.axis_index("tm"), attended_ref.shape[0])
    copy.wait()


def gathered_plan(
    hidden_states, first_gain, second_gain, query_weight, key_weight, value_weight, out_weight, conv_kernel
):
    frames, _, cols, channels = hidden_states.shape
    rows, blocks = lax.axis_size("space"), lax.axis_size("tm")
    own = hidden_states.reshape(frames * cols, channels)
    gains = (first_gain.reshape(1, channels), second_gain.reshape(1, channels))
    by_row = {row: exchange(own, "space", row) for row in range(rows - 1, 0, -1)}
    first = exchange(own, "tm", 1)
    onward = {row: exchange(piece, "tm", 1) for row, piece in by_row.items() if row >= rows // 2}
    for row in range(1, rows // 2):
        onward[row] = exchange(own, ("space", "tm"), row * blocks + 1)
    staged = (query_weight, key_weight, value_weight, out_weight, own, *gains, conv_kernel)
    *weights, in_out, own_out, own_staged, first_gain, second_gain, early_taps = stage(staged, by_row[rows // 2])
    near = [own_staged, first]
    for row in range(1, rows // 2):
        near += [by_row[row], onward[row]]
    far = [piece for row in range(rows // 2, rows) for piece in (by_row[row], onward[row])]
    near_mine = pack(near_kernel, near, "near", (first_gain, second_gain))
    near_other = exchange(near_mine, "chan", 1)
    far_mine = pack(pack_kernel, far, "far")
    far_other = exchange(far_mine, "chan", 1)
    in_channels, out_channels = conv_kernel.shape[3:]
    tokens = blocks * frames * rows * cols
    in_vmem = pl.BlockSpec(memory_space=pltpu.VMEM)
    *begun, last_tap = pl.pallas_call(
        functools.partial(mine_kernel, layout=(frames, cols, rows, blocks)),
        out_shape=(jax.ShapeDtypeStruct((tokens, D), jnp.float32),) * 3
        + (jax.ShapeDtypeStruct((1, *conv_kernel.shape[1:]), conv_kernel.dtype),),
        in_specs=[in_vmem] * 5 + [pl.BlockSpec(memory_space=pltpu.HBM)],
        out_specs=(in_vmem,) * 4,
        scratch_shapes=[pltpu.VMEM((tokens, channels), jnp.bfloat16), pltpu.SemaphoreType.DMA],
        compiler_params=pltpu.CompilerParams(vmem_limit_bytes=8 * 1024 * 1024),
        name="mine",
    )(near_mine, far_mine, *weights, in_hbm(conv_kernel))
    own_mixed, activated, send = pl.pallas_call(
        main_kernel,
        out_shape=(
            jax.ShapeDtypeStruct((frames * cols, D), jnp.bfloat16),
            jax.ShapeDtypeStruct((3, blocks * frames + 2, cols, in_channels), jnp.bfloat16),
            jax.ShapeDtypeStruct((frames * cols, out_channels), jnp.bfloat16),
        ),
        in_specs=[in_vmem] * 13,
        out_specs=(in_vmem,) * 3,
        scratch_shapes=[pltpu.VMEM((tokens, channels), jnp.bfloat16)]
        + [pltpu.VMEM((tokens, D), jnp.bfloat16)] * 4
        + [pltpu.VMEM((blocks * frames, rows, cols, in_channels), jnp.float32)]
        + [pltpu.VMEM((tokens, in_channels), jnp.bfloat16)],
        compiler_params=pltpu.CompilerParams(vmem_limit_bytes=24 * 1024 * 1024),
        name="block",
    )(near_mine, far_mine, near_other, far_other, *weights, *begun, in_out, early_taps, last_tap)
    received = exchange(send, "tm", 1)
    attended, keep = pl.pallas_call(
        own_kernel,
        out_shape=(
            jax.ShapeDtypeStruct((frames, 1, cols, channels), jnp.bfloat16),
            jax.ShapeDtypeStruct((frames * cols, out_channels), jnp.float32),
        ),
        in_specs=[in_vmem] * 5,
        out_specs=(pl.BlockSpec(memory_space=pl.ANY), in_vmem),
        scratch_shapes=[pltpu.VMEM((frames, 1, cols, channels), jnp.bfloat16), pltpu.SemaphoreType.DMA],
        compiler_params=pltpu.CompilerParams(vmem_limit_bytes=4 * 1024 * 1024),
        name="own",
    )(activated, early_taps, last_tap, own_mixed, own_out)
    total = keep + received.astype(jnp.float32)
    return attended, total.astype(jnp.bfloat16).reshape(frames, 1, cols, out_channels)


def power_of_two(count):
    return count & (count - 1) == 0


def on_device(hidden_states, *others):
    frames, rows, cols, channels = hidden_states.shape
    spaces, blocks = lax.axis_size("space"), lax.axis_size("tm")
    tokens = frames * blocks * spaces * rows * cols
    fits = tokens * D <= 2 ** 20 and rows == 1 and lax.axis_size("chan") == 2 and blocks == 2
    if fits and power_of_two(spaces):
        return gathered_plan(hidden_states, *others)
    return split_plan(hidden_states, *others)


def solution(mesh):
    placed = (
        P(("groups", "tm"), "space", None, "chan"),
        P("chan"),
        P("chan"),
        P(),
        P(),
        P(),
        P(),
        P(None, None, None, "tm", "chan"),
    )
    return jax.shard_map(
        on_device,
        mesh=mesh,
        in_specs=placed,
        out_specs=(
            P(("groups", "tm"), "space", None, "chan"),
            P(("groups", "tm"), "space", None, "chan"),
        ),
        check_vma=False,
    )
```

```python
import functools

import jax
import jax.numpy as jnp
from jax import lax
from jax.experimental import pallas as pl
from jax.experimental.pallas import tpu as pltpu
from jax.sharding import PartitionSpec as P

D = 512
NGROUP = 32


EPSILON = 1e-06


def shifted_2(x, axis, by):
    peers = lax.axis_size(axis)
    pairs = [(i, i + by) for i in range(peers) if 0 <= i + by < peers]
    return lax.ppermute(x, axis, pairs)


def padded_2(cells, sides, width):
    for axis, dim in sides:
        count = lax.axis_size(axis)
        ends = count - 1
        head = lax.slice_in_dim(cells, 0, width, axis=dim)
        tail = lax.slice_in_dim(cells, cells.shape[dim] - width, cells.shape[dim], axis=dim)
        cells = jnp.concatenate(
            [
                lax.ppermute(tail, axis, [(i, (i + 1) % count) for i in range(ends)]),
                cells,
                lax.ppermute(head, axis, [((i + 1) % count, i) for i in range(ends)]),
            ],
            axis=dim,
        )
    return cells


def normalize(source, gain_vector):
    channels = source.shape[3]
    group_width = D // NGROUP
    grouped = source.reshape(-1, channels // group_width, group_width)
    population = grouped.shape[0] * group_width * lax.axis_size("space") * lax.axis_size("tm")
    group_sums, group_squares = lax.psum(
        (jnp.sum(grouped, axis=(0, 2)), jnp.sum(grouped * grouped, axis=(0, 2))), ("space", "tm")
    )
    centre = group_sums / population
    spread = jnp.maximum(group_squares / population - centre * centre, 0.0)
    shifted = grouped - centre[None, :, None]
    scaled = shifted * lax.rsqrt(spread + EPSILON)[None, :, None]
    return scaled.reshape(source.shape) * gain_vector


def attend(normed, query_weight, key_weight, value_weight, out_weight):
    frame_count, row_count, col_count, channels = normed.shape
    token_count = frame_count * row_count * col_count
    tokens = normed.reshape(token_count, channels)
    halves = lax.all_to_all(tokens, "chan", split_axis=0, concat_axis=1, tiled=True)
    half_rows = halves.shape[0]
    queries = jnp.dot(halves, query_weight, preferred_element_type=jnp.float32).astype(jnp.bfloat16)
    keyed = jnp.dot(halves, key_weight, preferred_element_type=jnp.float32).astype(jnp.bfloat16)
    valued = jnp.dot(halves, value_weight, preferred_element_type=jnp.float32).astype(jnp.bfloat16)
    score_scale = D ** (-0.5)
    running_max = jnp.full((half_rows,), -1e30, jnp.float32)
    key_piece = lax.all_gather(keyed, "space", axis=0, tiled=True)
    value_piece = lax.all_gather(valued, "space", axis=0, tiled=True)
    scores = jnp.dot(queries, key_piece.T, preferred_element_type=jnp.float32) * score_scale
    newest_max = jnp.maximum(running_max, jnp.max(scores, axis=1))
    weights = jnp.exp(scores - newest_max[:, None])
    running_sum = jnp.sum(weights, axis=1)
    accumulated = jnp.dot(
        weights.astype(jnp.bfloat16), value_piece, preferred_element_type=jnp.float32
    )
    mixed = (accumulated / running_sum[:, None]).astype(jnp.bfloat16)
    projected = jnp.dot(mixed, out_weight, preferred_element_type=jnp.float32).astype(jnp.bfloat16)
    returned = lax.all_to_all(projected, "chan", split_axis=1, concat_axis=0, tiled=True)
    return returned.reshape(frame_count, row_count, col_count, channels)


def join_channels(activated):
    return lax.all_gather(activated, "chan", axis=3, tiled=True)


def extend(frames_in):
    earlier = shifted_2(frames_in, "tm", 1)
    timed = jnp.concatenate([earlier, frames_in], axis=0)
    rimmed = padded_2(timed, (("space", 1),), 1)
    return jnp.pad(rimmed, ((0, 0), (0, 0), (1, 1), (0, 0)))


def convolve(activated, conv_kernel):
    frame_count, row_count, col_count = (activated.shape[0], activated.shape[1], activated.shape[2])
    padded = extend(join_channels(activated))
    out_width = conv_kernel.shape[4]
    initial = jnp.zeros((frame_count * row_count * col_count, out_width), jnp.float32)
    running_total = initial
    piece = lax.all_gather(conv_kernel, "tm", axis=3, tiled=True)
    for time_tap in range(3):
        for row_tap in range(3):
            for col_tap in range(3):
                window = padded[
                    time_tap : time_tap + frame_count,
                    row_tap : row_tap + row_count,
                    col_tap : col_tap + col_count,
                ]
                window = window.reshape(frame_count * row_count * col_count, piece.shape[3])
                running_total = running_total + jnp.dot(
                    window, piece[time_tap, row_tap, col_tap], preferred_element_type=jnp.float32
                )
    return running_total.reshape(frame_count, row_count, col_count, out_width).astype(jnp.bfloat16)


def split_plan(
    hidden_states,
    first_gain,
    second_gain,
    query_weight,
    key_weight,
    value_weight,
    out_weight,
    conv_kernel,
):
    source = hidden_states.astype(jnp.float32)
    normed = normalize(source, first_gain).astype(jnp.bfloat16)
    attended = attend(normed, query_weight, key_weight, value_weight, out_weight)
    resid = source + attended.astype(jnp.float32)
    activated = jax.nn.silu(normalize(resid, second_gain)).astype(jnp.bfloat16)
    convolved = convolve(activated, conv_kernel)
    return (attended, convolved)


GAIN_ROWS = 16


def exchange(x, axes, step):
    peers = lax.axis_size(axes)
    return lax.ppermute(x, axes, [(i, i ^ step) for i in range(peers)])


def stage_kernel(
    query_hbm, key_hbm, value_hbm, out_weight_hbm, own_hbm, first_hbm, second_hbm, kernel_hbm, _,
    query_ref, key_ref, value_ref, in_out_ref, own_out_ref, own_ref, first_ref, second_ref, tap_ref, arrived,
):
    channels, in_channels = own_out_ref.shape[1], in_out_ref.shape[1]
    own_half = pl.ds(pl.multiple_of(lax.axis_index("chan") * channels, channels), channels)
    in_half = pl.ds(pl.multiple_of(lax.axis_index("tm") * in_channels, in_channels), in_channels)
    moves = []
    other_half = pl.ds(pl.multiple_of((1 - lax.axis_index("chan")) * channels, channels), channels)
    for source, target in ((query_hbm, query_ref), (key_hbm, key_ref), (value_hbm, value_ref)):
        moves.append((source.at[own_half], target.at[pl.ds(0, channels)]))
        moves.append((source.at[other_half], target.at[pl.ds(channels, channels)]))
    moves += [
        (out_weight_hbm.at[:, in_half], in_out_ref), (out_weight_hbm.at[:, own_half], own_out_ref),
        (own_hbm, own_ref), (first_hbm, first_ref), (second_hbm, second_ref), (kernel_hbm.at[pl.ds(0, tap_ref.shape[0])], tap_ref),
    ]
    copies = [pltpu.make_async_copy(*move, arrived.at[place]) for place, move in enumerate(moves)]
    for copy in copies:
        copy.start()
    for copy in copies:
        copy.wait()


def stage(arrays, after):
    query_weight, _, _, out_weight, own, first_gain, second_gain, conv_kernel = arrays
    in_channels = conv_kernel.shape[3]
    shapes = [query_weight.shape] * 3 + [(out_weight.shape[0], in_channels), (out_weight.shape[0], own.shape[1])]
    shapes = [jax.ShapeDtypeStruct(shape, own.dtype) for shape in shapes + [own.shape, (conv_kernel.shape[0] - 1, *conv_kernel.shape[1:])]]
    gains = [jax.ShapeDtypeStruct(gain.shape, gain.dtype) for gain in (first_gain, second_gain)]
    shapes = shapes[:-1] + gains + shapes[-1:]
    return pl.pallas_call(
        stage_kernel,
        out_shape=tuple(shapes),
        in_specs=[pl.BlockSpec(memory_space=pltpu.HBM)] * len(arrays) + [pl.BlockSpec(memory_space=pl.ANY)],
        out_specs=tuple(pl.BlockSpec(memory_space=pltpu.VMEM) for _ in shapes),
        scratch_shapes=[pltpu.SemaphoreType.DMA((12,))],
        compiler_params=pltpu.CompilerParams(vmem_limit_bytes=1 << 20),
        name="stage",
    )(*(in_hbm(array) for array in arrays), after)


def pack_kernel(*refs):
    end = 0
    for piece_ref in refs[:-1]:
        start, end = end, end + piece_ref.shape[0]
        refs[-1][start:end, :] = piece_ref[...]


def near_kernel(first_ref, second_ref, *refs):
    pack_kernel(*refs)
    parts = split_parts(first_ref[...]) + split_parts(second_ref[...])
    parts = [part.astype(jnp.float32) for part in parts]
    parts.append(jnp.zeros((GAIN_ROWS - len(parts), first_ref.shape[1]), jnp.float32))
    end = refs[-1].shape[0]
    refs[-1][end - GAIN_ROWS : end, :] = jnp.concatenate(parts, axis=0).astype(jnp.bfloat16)


def pack(kernel, pieces, name, gains=()):
    size = sum(piece.shape[0] for piece in pieces) + (GAIN_ROWS if gains else 0)
    return pl.pallas_call(
        kernel,
        out_shape=jax.ShapeDtypeStruct((size, pieces[0].shape[1]), pieces[0].dtype),
        compiler_params=pltpu.CompilerParams(vmem_limit_bytes=2 * 1024 * 1024),
        name=name,
    )(*gains, *pieces)


def in_hbm(array):
    return pltpu.with_memory_space_constraint(array, pltpu.HBM)


def split_parts(values):
    parts = []
    for _ in range(3):
        rounded = values.astype(jnp.bfloat16)
        parts.append(rounded)
        values = values - rounded.astype(jnp.float32)
    return parts


def group_statistics(rows, count):
    channels = rows[0].shape[1]
    width = D // NGROUP
    left = lax.broadcasted_iota(jnp.int32, (channels, channels), 0) // width
    right = lax.broadcasted_iota(jnp.int32, (channels, channels), 1) // width
    member = jnp.where(left == right, 1.0, 0.0).astype(jnp.bfloat16)
    parts = [part for row in rows for part in split_parts(row)]
    parts += [jnp.zeros((1, channels), jnp.bfloat16)] * (16 - len(parts))
    totals = jnp.dot(jnp.concatenate(parts, axis=0), member, preferred_element_type=jnp.float32)
    means = [
        (totals[at : at + 1] + totals[at + 1 : at + 2] + totals[at + 2 : at + 3]) * (1.0 / count)
        for at in range(0, 3 * len(rows), 3)
    ]
    found = []
    for centre, square in zip(means[::2], means[1::2]):
        spread = jnp.maximum(square - centre * centre, 0.0)
        found.append((centre, lax.rsqrt(spread + EPSILON)))
    return found


def core_chunks(near, far, layout):
    own_frames, cols, rows, blocks = layout
    size = own_frames * cols
    places = [(ref, at) for ref in (near, far) for at in range(0, ref.shape[0] - size + 1, size)]
    chunks = []
    for index in range(blocks):
        for frame in range(own_frames):
            for row in range(rows):
                ref, at = places[row * blocks + index]
                chunks.append((ref, slice(at + frame * cols, at + (frame + 1) * cols)))
    return chunks


def core_gain(near, which):
    end = near.shape[0]
    parts = near[end - GAIN_ROWS : end, :].astype(jnp.float32)
    at = 3 * which
    return parts[at : at + 1] + parts[at + 1 : at + 2] + parts[at + 2 : at + 3]


def add_chunk(totals, values):
    parts = values.reshape(values.shape[0] // 8, 8, values.shape[1])
    found = [jnp.sum(parts, axis=0), jnp.sum(parts * parts, axis=0)]
    return found if totals is None else [total + part for total, part in zip(totals, found)]


def chunk_statistics(totals, count):
    ((centre, scale),) = group_statistics([jnp.sum(total, axis=0, keepdims=True) for total in totals], count)
    return centre, scale


def norm_chunks(chunks, gain, normed):
    totals = None
    for ref, at in chunks:
        totals = add_chunk(totals, ref[at, :].astype(jnp.float32))
    centre, scale = chunk_statistics(totals, normed.shape[0] * (D // NGROUP))
    scale = scale * gain
    end = 0
    for ref, at in chunks:
        start, end = end, end + at.stop - at.start
        normed[start:end, :] = ((ref[at, :].astype(jnp.float32) - centre) * scale).astype(jnp.bfloat16)


def mine_kernel(
    near_ref, far_ref, query_ref, key_ref, value_ref, kernel_hbm,
    begun_query, begun_key, begun_value, last_tap, normed, arrived, *, layout,
):
    copy = pltpu.make_async_copy(kernel_hbm.at[pl.ds(kernel_hbm.shape[0] - 1, 1)], last_tap, arrived)
    copy.start()
    norm_chunks(core_chunks(near_ref, far_ref, layout), core_gain(near_ref, 0), normed)
    channels = normed.shape[1]
    for weight_ref, target in zip((query_ref, key_ref, value_ref), (begun_query, begun_key, begun_value)):
        target[...] = jnp.dot(normed[...], weight_ref[:channels, :], preferred_element_type=jnp.float32)
    copy.wait()


def main_kernel(
    near_ref, far_ref, other_near_ref, other_far_ref, query_ref, key_ref, value_ref, begun_query, begun_key, begun_value,
    in_out_ref, early_taps, last_tap,
    own_mixed, activated, send_ref,
    normed, queries, keyed, valued, mixed, resid, projected,
):
    frames, rows, cols, channels = resid.shape
    own_frames = own_mixed.shape[0] // cols
    tokens = frames * rows * cols
    frame_tokens = rows * cols
    space = lax.axis_index("space")
    block = lax.axis_index("tm")
    half = lax.axis_index("chan")
    width = D // NGROUP
    count = tokens * width

    blocks = frames // own_frames

    layout = (own_frames, cols, rows, blocks)
    mine, other = core_chunks(near_ref, far_ref, layout), core_chunks(other_near_ref, other_far_ref, layout)
    norm_chunks(other, core_gain(other_near_ref, 0), normed)
    in_channels = early_taps.shape[3]
    mine_in = block == half
    spans = [slice(frame * frame_tokens, (frame + 1) * frame_tokens) for frame in range(frames)]
    for weight_ref, begun_ref, target in ((query_ref, begun_query, queries), (key_ref, begun_key, keyed)):
        term = jnp.dot(normed[...], weight_ref[channels:, :], preferred_element_type=jnp.float32)
        target[...] = (begun_ref[...] + term).astype(jnp.bfloat16)
    scores = [
        lax.dot_general(queries[at, :], keyed[at, :], (((1,), (1,)), ((), ())), preferred_element_type=jnp.float32)
        for at in spans
    ]
    for weight_ref, begun_ref, target in ((value_ref, begun_value, valued),):
        term = jnp.dot(normed[...], weight_ref[channels:, :], preferred_element_type=jnp.float32)
        target[...] = (begun_ref[...] + term).astype(jnp.bfloat16)
    for at, score in zip(spans, scores):
        peak = jnp.max(score, axis=1, keepdims=True)
        weights = jnp.exp((score - peak) * (D ** (-0.5)))
        mass = jnp.sum(weights, axis=1, keepdims=True)
        blend = jnp.dot(weights.astype(jnp.bfloat16), valued[at, :], preferred_element_type=jnp.float32)
        mixed[at, :] = (blend * (1.0 / mass)).astype(jnp.bfloat16)
    projected[...] = jnp.dot(mixed[...], in_out_ref[...], preferred_element_type=jnp.float32).astype(jnp.bfloat16)
    totals = None
    for chunk, ((ref, at), (other_ref, _)) in enumerate(zip(mine, other)):
        source = jnp.where(mine_in, ref[at, :], other_ref[at, :]).astype(jnp.float32)
        total = source + projected[chunk * cols : (chunk + 1) * cols, :].astype(jnp.float32)
        resid[chunk // rows, chunk % rows] = total
        totals = add_chunk(totals, total)
    size = own_mixed.shape[0] // own_frames
    for frame, at in enumerate(spans[:own_frames]):
        own_mixed[frame * size : (frame + 1) * size, :] = mixed[at.start : at.start + size, :]

    centre, scale = chunk_statistics(totals, count)
    scale = 0.5 * scale * jnp.where(mine_in, core_gain(near_ref, 1), core_gain(other_near_ref, 1))
    activated[:, 0:2] = jnp.zeros((3, 2, cols, in_channels), jnp.bfloat16)
    for tap in range(3):
        row = space + (tap - 1)
        inside = jnp.logical_and(row >= 0, row < rows)
        place = jnp.where(inside, space ^ row, 0)
        row_scale = jnp.where(inside, scale, 0.0)
        for frame in range(frames):
            relative = ((frame // own_frames) ^ block) * own_frames + frame % own_frames
            halved = (resid[relative, place] - centre) * row_scale
            activated[tap, frame + 2] = (halved + halved * jnp.tanh(halved)).astype(jnp.bfloat16)

    send_ref[...] = partial_conv(activated, early_taps, last_tap, 1 - block, own_frames).astype(jnp.bfloat16)


def partial_conv(activated, early_taps, last_tap, block, frames):
    cols, in_channels = activated.shape[2:]
    tokens = frames * cols
    taps = [ref.at[tap] for ref in (early_taps, last_tap) for tap in range(ref.shape[0])]
    columns = []
    for col_tap in range(3):
        total = None
        for time_tap in range(3):
            start = block * frames + time_tap
            windows = [activated[row_tap, pl.ds(start, frames)].reshape(tokens, in_channels) for row_tap in range(3)]
            term = jnp.dot(
                jnp.concatenate(windows, axis=1),
                taps[time_tap][:, col_tap].reshape(3 * in_channels, -1),
                preferred_element_type=jnp.float32,
            )
            total = term if total is None else total + term
        columns.append(total)
    place = lax.broadcasted_iota(jnp.int32, columns[0].shape, 0) % cols
    left = jnp.where(place == 0, 0.0, pltpu.roll(columns[0], 1, 0))
    right = jnp.where(place == cols - 1, 0.0, pltpu.roll(columns[2], tokens - 1, 0))
    return columns[1] + left + right


def own_kernel(activated, early_taps, last_tap, own_mixed, own_out_ref, attended_hbm, keep_ref, attended_ref, sent):
    attended_ref[...] = jnp.dot(
        own_mixed[...], own_out_ref[...], preferred_element_type=jnp.float32
    ).astype(jnp.bfloat16).reshape(attended_ref.shape)
    copy = pltpu.make_async_copy(attended_ref, attended_hbm, sent)
    copy.start()
    keep_ref[...] = partial_conv(activated, early_taps, last_tap, lax.axis_index("tm"), attended_ref.shape[0])
    copy.wait()


def gathered_plan(
    hidden_states, first_gain, second_gain, query_weight, key_weight, value_weight, out_weight, conv_kernel
):
    frames, _, cols, channels = hidden_states.shape
    rows, blocks = lax.axis_size("space"), lax.axis_size("tm")
    own = hidden_states.reshape(frames * cols, channels)
    gains = (first_gain.reshape(1, channels), second_gain.reshape(1, channels))
    by_row = {row: exchange(own, "space", row) for row in range(rows - 1, 0, -1)}
    first = exchange(own, "tm", 1)
    onward = {row: exchange(piece, "tm", 1) for row, piece in by_row.items() if row >= rows // 2}
    for row in range(1, rows // 2):
        onward[row] = exchange(own, ("space", "tm"), row * blocks + 1)
    staged = (query_weight, key_weight, value_weight, out_weight, own, *gains, conv_kernel)
    *weights, in_out, own_out, own_staged, first_gain, second_gain, early_taps = stage(staged, by_row[rows - 1])
    near = [own_staged, first]
    for row in range(1, rows // 2):
        near += [by_row[row], onward[row]]
    far = [piece for row in range(rows // 2, rows) for piece in (by_row[row], onward[row])]
    near_mine = pack(near_kernel, near, "near", (first_gain, second_gain))
    near_other = exchange(near_mine, "chan", 1)
    far_mine = pack(pack_kernel, far, "far")
    far_other = exchange(far_mine, "chan", 1)
    in_channels, out_channels = conv_kernel.shape[3:]
    tokens = blocks * frames * rows * cols
    in_vmem = pl.BlockSpec(memory_space=pltpu.VMEM)
    *begun, last_tap = pl.pallas_call(
        functools.partial(mine_kernel, layout=(frames, cols, rows, blocks)),
        out_shape=(jax.ShapeDtypeStruct((tokens, D), jnp.float32),) * 3
        + (jax.ShapeDtypeStruct((1, *conv_kernel.shape[1:]), conv_kernel.dtype),),
        in_specs=[in_vmem] * 5 + [pl.BlockSpec(memory_space=pltpu.HBM)],
        out_specs=(in_vmem,) * 4,
        scratch_shapes=[pltpu.VMEM((tokens, channels), jnp.bfloat16), pltpu.SemaphoreType.DMA],
        compiler_params=pltpu.CompilerParams(vmem_limit_bytes=8 * 1024 * 1024),
        name="mine",
    )(near_mine, far_mine, *weights, in_hbm(conv_kernel))
    own_mixed, activated, send = pl.pallas_call(
        main_kernel,
        out_shape=(
            jax.ShapeDtypeStruct((frames * cols, D), jnp.bfloat16),
            jax.ShapeDtypeStruct((3, blocks * frames + 2, cols, in_channels), jnp.bfloat16),
            jax.ShapeDtypeStruct((frames * cols, out_channels), jnp.bfloat16),
        ),
        in_specs=[in_vmem] * 13,
        out_specs=(in_vmem,) * 3,
        scratch_shapes=[pltpu.VMEM((tokens, channels), jnp.bfloat16)]
        + [pltpu.VMEM((tokens, D), jnp.bfloat16)] * 4
        + [pltpu.VMEM((blocks * frames, rows, cols, in_channels), jnp.float32)]
        + [pltpu.VMEM((tokens, in_channels), jnp.bfloat16)],
        compiler_params=pltpu.CompilerParams(vmem_limit_bytes=24 * 1024 * 1024),
        name="block",
    )(near_mine, far_mine, near_other, far_other, *weights, *begun, in_out, early_taps, last_tap)
    received = exchange(send, "tm", 1)
    attended, keep = pl.pallas_call(
        own_kernel,
        out_shape=(
            jax.ShapeDtypeStruct((frames, 1, cols, channels), jnp.bfloat16),
            jax.ShapeDtypeStruct((frames * cols, out_channels), jnp.float32),
        ),
        in_specs=[in_vmem] * 5,
        out_specs=(pl.BlockSpec(memory_space=pl.ANY), in_vmem),
        scratch_shapes=[pltpu.VMEM((frames, 1, cols, channels), jnp.bfloat16), pltpu.SemaphoreType.DMA],
        compiler_params=pltpu.CompilerParams(vmem_limit_bytes=4 * 1024 * 1024),
        name="own",
    )(activated, early_taps, last_tap, own_mixed, own_out)
    total = keep + received.astype(jnp.float32)
    return attended, total.astype(jnp.bfloat16).reshape(frames, 1, cols, out_channels)


def power_of_two(count):
    return count & (count - 1) == 0


def on_device(hidden_states, *others):
    frames, rows, cols, channels = hidden_states.shape
    spaces, blocks = lax.axis_size("space"), lax.axis_size("tm")
    tokens = frames * blocks * spaces * rows * cols
    fits = tokens * D <= 2 ** 20 and rows == 1 and lax.axis_size("chan") == 2 and blocks == 2
    if fits and power_of_two(spaces):
        return gathered_plan(hidden_states, *others)
    return split_plan(hidden_states, *others)


def solution(mesh):
    placed = (
        P(("groups", "tm"), "space", None, "chan"),
        P("chan"),
        P("chan"),
        P(),
        P(),
        P(),
        P(),
        P(None, None, None, "tm", "chan"),
    )
    return jax.shard_map(
        on_device,
        mesh=mesh,
        in_specs=placed,
        out_specs=(
            P(("groups", "tm"), "space", None, "chan"),
            P(("groups", "tm"), "space", None, "chan"),
        ),
        check_vma=False,
    )
```

```python
import functools

import jax
import jax.numpy as jnp
from jax import lax
from jax.experimental import pallas as pl
from jax.experimental.pallas import tpu as pltpu
from jax.sharding import PartitionSpec as P

D = 512
NGROUP = 32


EPSILON = 1e-06
LOG2_E = 1.4426950408889634


def shifted_2(x, axis, by):
    peers = lax.axis_size(axis)
    pairs = [(i, i + by) for i in range(peers) if 0 <= i + by < peers]
    return lax.ppermute(x, axis, pairs)


def padded_2(cells, sides, width):
    for axis, dim in sides:
        count = lax.axis_size(axis)
        ends = count - 1
        head = lax.slice_in_dim(cells, 0, width, axis=dim)
        tail = lax.slice_in_dim(cells, cells.shape[dim] - width, cells.shape[dim], axis=dim)
        cells = jnp.concatenate(
            [
                lax.ppermute(tail, axis, [(i, (i + 1) % count) for i in range(ends)]),
                cells,
                lax.ppermute(head, axis, [((i + 1) % count, i) for i in range(ends)]),
            ],
            axis=dim,
        )
    return cells


def normalize(source, gain_vector):
    channels = source.shape[3]
    group_width = D // NGROUP
    grouped = source.reshape(-1, channels // group_width, group_width)
    population = grouped.shape[0] * group_width * lax.axis_size("space") * lax.axis_size("tm")
    group_sums, group_squares = lax.psum(
        (jnp.sum(grouped, axis=(0, 2)), jnp.sum(grouped * grouped, axis=(0, 2))), ("space", "tm")
    )
    centre = group_sums / population
    spread = jnp.maximum(group_squares / population - centre * centre, 0.0)
    shifted = grouped - centre[None, :, None]
    scaled = shifted * lax.rsqrt(spread + EPSILON)[None, :, None]
    return scaled.reshape(source.shape) * gain_vector


def attend(normed, query_weight, key_weight, value_weight, out_weight):
    frame_count, row_count, col_count, channels = normed.shape
    token_count = frame_count * row_count * col_count
    tokens = normed.reshape(token_count, channels)
    halves = lax.all_to_all(tokens, "chan", split_axis=0, concat_axis=1, tiled=True)
    half_rows = halves.shape[0]
    queries = jnp.dot(halves, query_weight, preferred_element_type=jnp.float32).astype(jnp.bfloat16)
    keyed = jnp.dot(halves, key_weight, preferred_element_type=jnp.float32).astype(jnp.bfloat16)
    valued = jnp.dot(halves, value_weight, preferred_element_type=jnp.float32).astype(jnp.bfloat16)
    score_scale = D ** (-0.5)
    running_max = jnp.full((half_rows,), -1e30, jnp.float32)
    key_piece = lax.all_gather(keyed, "space", axis=0, tiled=True)
    value_piece = lax.all_gather(valued, "space", axis=0, tiled=True)
    scores = jnp.dot(queries, key_piece.T, preferred_element_type=jnp.float32) * score_scale
    newest_max = jnp.maximum(running_max, jnp.max(scores, axis=1))
    weights = jnp.exp(scores - newest_max[:, None])
    running_sum = jnp.sum(weights, axis=1)
    accumulated = jnp.dot(
        weights.astype(jnp.bfloat16), value_piece, preferred_element_type=jnp.float32
    )
    mixed = (accumulated / running_sum[:, None]).astype(jnp.bfloat16)
    projected = jnp.dot(mixed, out_weight, preferred_element_type=jnp.float32).astype(jnp.bfloat16)
    returned = lax.all_to_all(projected, "chan", split_axis=1, concat_axis=0, tiled=True)
    return returned.reshape(frame_count, row_count, col_count, channels)


def join_channels(activated):
    return lax.all_gather(activated, "chan", axis=3, tiled=True)


def extend(frames_in):
    earlier = shifted_2(frames_in, "tm", 1)
    timed = jnp.concatenate([earlier, frames_in], axis=0)
    rimmed = padded_2(timed, (("space", 1),), 1)
    return jnp.pad(rimmed, ((0, 0), (0, 0), (1, 1), (0, 0)))


def convolve(activated, conv_kernel):
    frame_count, row_count, col_count = (activated.shape[0], activated.shape[1], activated.shape[2])
    padded = extend(join_channels(activated))
    out_width = conv_kernel.shape[4]
    initial = jnp.zeros((frame_count * row_count * col_count, out_width), jnp.float32)
    running_total = initial
    piece = lax.all_gather(conv_kernel, "tm", axis=3, tiled=True)
    for time_tap in range(3):
        for row_tap in range(3):
            for col_tap in range(3):
                window = padded[
                    time_tap : time_tap + frame_count,
                    row_tap : row_tap + row_count,
                    col_tap : col_tap + col_count,
                ]
                window = window.reshape(frame_count * row_count * col_count, piece.shape[3])
                running_total = running_total + jnp.dot(
                    window, piece[time_tap, row_tap, col_tap], preferred_element_type=jnp.float32
                )
    return running_total.reshape(frame_count, row_count, col_count, out_width).astype(jnp.bfloat16)


def split_plan(
    hidden_states,
    first_gain,
    second_gain,
    query_weight,
    key_weight,
    value_weight,
    out_weight,
    conv_kernel,
):
    source = hidden_states.astype(jnp.float32)
    normed = normalize(source, first_gain).astype(jnp.bfloat16)
    attended = attend(normed, query_weight, key_weight, value_weight, out_weight)
    resid = source + attended.astype(jnp.float32)
    activated = jax.nn.silu(normalize(resid, second_gain)).astype(jnp.bfloat16)
    convolved = convolve(activated, conv_kernel)
    return (attended, convolved)


GAIN_ROWS = 16


def exchange(x, axes, step):
    peers = lax.axis_size(axes)
    return lax.ppermute(x, axes, [(i, i ^ step) for i in range(peers)])


def stage_kernel(
    query_hbm, key_hbm, value_hbm, out_weight_hbm, own_hbm, first_hbm, second_hbm, kernel_hbm, _,
    query_ref, key_ref, value_ref, in_out_ref, own_out_ref, own_ref, first_ref, second_ref, tap_ref, arrived,
):
    channels, in_channels = own_out_ref.shape[1], in_out_ref.shape[1]
    own_half = pl.ds(pl.multiple_of(lax.axis_index("chan") * channels, channels), channels)
    in_half = pl.ds(pl.multiple_of(lax.axis_index("tm") * in_channels, in_channels), in_channels)
    moves = []
    other_half = pl.ds(pl.multiple_of((1 - lax.axis_index("chan")) * channels, channels), channels)
    for source, target in ((query_hbm, query_ref), (key_hbm, key_ref), (value_hbm, value_ref)):
        moves.append((source.at[own_half], target.at[pl.ds(0, channels)]))
        moves.append((source.at[other_half], target.at[pl.ds(channels, channels)]))
    moves += [
        (out_weight_hbm.at[:, in_half], in_out_ref), (out_weight_hbm.at[:, own_half], own_out_ref),
        (own_hbm, own_ref), (first_hbm, first_ref), (second_hbm, second_ref), (kernel_hbm.at[pl.ds(0, tap_ref.shape[0])], tap_ref),
    ]
    copies = [pltpu.make_async_copy(*move, arrived.at[place]) for place, move in enumerate(moves)]
    for copy in copies:
        copy.start()
    for copy in copies:
        copy.wait()


def stage(arrays, after):
    query_weight, _, _, out_weight, own, first_gain, second_gain, conv_kernel = arrays
    in_channels = conv_kernel.shape[3]
    shapes = [query_weight.shape] * 3 + [(out_weight.shape[0], in_channels), (out_weight.shape[0], own.shape[1])]
    shapes = [jax.ShapeDtypeStruct(shape, own.dtype) for shape in shapes + [own.shape, (conv_kernel.shape[0] - 1, *conv_kernel.shape[1:])]]
    gains = [jax.ShapeDtypeStruct(gain.shape, gain.dtype) for gain in (first_gain, second_gain)]
    shapes = shapes[:-1] + gains + shapes[-1:]
    return pl.pallas_call(
        stage_kernel,
        out_shape=tuple(shapes),
        in_specs=[pl.BlockSpec(memory_space=pltpu.HBM)] * len(arrays) + [pl.BlockSpec(memory_space=pl.ANY)],
        out_specs=tuple(pl.BlockSpec(memory_space=pltpu.VMEM) for _ in shapes),
        scratch_shapes=[pltpu.SemaphoreType.DMA((12,))],
        compiler_params=pltpu.CompilerParams(vmem_limit_bytes=1 << 20),
        name="stage",
    )(*(in_hbm(array) for array in arrays), after)


def pack_kernel(*refs):
    end = 0
    for piece_ref in refs[:-1]:
        start, end = end, end + piece_ref.shape[0]
        refs[-1][start:end, :] = piece_ref[...]


def near_kernel(first_ref, second_ref, *refs):
    pack_kernel(*refs)
    parts = split_parts(first_ref[...]) + split_parts(second_ref[...])
    parts = [part.astype(jnp.float32) for part in parts]
    parts.append(jnp.zeros((GAIN_ROWS - len(parts), first_ref.shape[1]), jnp.float32))
    end = refs[-1].shape[0]
    refs[-1][end - GAIN_ROWS : end, :] = jnp.concatenate(parts, axis=0).astype(jnp.bfloat16)


def pack(kernel, pieces, name, gains=()):
    size = sum(piece.shape[0] for piece in pieces) + (GAIN_ROWS if gains else 0)
    return pl.pallas_call(
        kernel,
        out_shape=jax.ShapeDtypeStruct((size, pieces[0].shape[1]), pieces[0].dtype),
        compiler_params=pltpu.CompilerParams(vmem_limit_bytes=2 * 1024 * 1024),
        name=name,
    )(*gains, *pieces)


def in_hbm(array):
    return pltpu.with_memory_space_constraint(array, pltpu.HBM)


def split_parts(values):
    parts = []
    for _ in range(3):
        rounded = values.astype(jnp.bfloat16)
        parts.append(rounded)
        values = values - rounded.astype(jnp.float32)
    return parts


def group_statistics(rows, count):
    channels = rows[0].shape[1]
    width = D // NGROUP
    left = lax.broadcasted_iota(jnp.int32, (channels, channels), 0) // width
    right = lax.broadcasted_iota(jnp.int32, (channels, channels), 1) // width
    member = jnp.where(left == right, 1.0, 0.0).astype(jnp.bfloat16)
    parts = [part for row in rows for part in split_parts(row)]
    parts += [jnp.zeros((1, channels), jnp.bfloat16)] * (16 - len(parts))
    totals = jnp.dot(jnp.concatenate(parts, axis=0), member, preferred_element_type=jnp.float32)
    means = [
        (totals[at : at + 1] + totals[at + 1 : at + 2] + totals[at + 2 : at + 3]) * (1.0 / count)
        for at in range(0, 3 * len(rows), 3)
    ]
    found = []
    for centre, square in zip(means[::2], means[1::2]):
        spread = jnp.maximum(square - centre * centre, 0.0)
        found.append((centre, lax.rsqrt(spread + EPSILON)))
    return found


def core_chunks(near, far, layout):
    own_frames, cols, rows, blocks = layout
    size = own_frames * cols
    places = [(ref, at) for ref in (near, far) for at in range(0, ref.shape[0] - size + 1, size)]
    chunks = []
    for index in range(blocks):
        for frame in range(own_frames):
            for row in range(rows):
                ref, at = places[row * blocks + index]
                chunks.append((ref, slice(at + frame * cols, at + (frame + 1) * cols)))
    return chunks


def core_gain(near, which):
    end = near.shape[0]
    parts = near[end - GAIN_ROWS : end, :].astype(jnp.float32)
    at = 3 * which
    return parts[at : at + 1] + parts[at + 1 : at + 2] + parts[at + 2 : at + 3]


def add_chunk(totals, values):
    parts = values.reshape(values.shape[0] // 8, 8, values.shape[1])
    found = [jnp.sum(parts, axis=0), jnp.sum(parts * parts, axis=0)]
    return found if totals is None else [total + part for total, part in zip(totals, found)]


def chunk_statistics(totals, count):
    ((centre, scale),) = group_statistics([jnp.sum(total, axis=0, keepdims=True) for total in totals], count)
    return centre, scale


def norm_chunks(chunks, gain, normed):
    totals = None
    for ref, at in chunks:
        totals = add_chunk(totals, ref[at, :].astype(jnp.float32))
    centre, scale = chunk_statistics(totals, normed.shape[0] * (D // NGROUP))
    scale = scale * gain
    end = 0
    for ref, at in chunks:
        start, end = end, end + at.stop - at.start
        normed[start:end, :] = ((ref[at, :].astype(jnp.float32) - centre) * scale).astype(jnp.bfloat16)


def mine_kernel(
    near_ref, far_ref, query_ref, key_ref, value_ref, kernel_hbm,
    begun_query, begun_key, begun_value, last_tap, normed, arrived, *, layout,
):
    copy = pltpu.make_async_copy(kernel_hbm.at[pl.ds(kernel_hbm.shape[0] - 1, 1)], last_tap, arrived)
    copy.start()
    norm_chunks(core_chunks(near_ref, far_ref, layout), core_gain(near_ref, 0), normed)
    channels = normed.shape[1]
    for weight_ref, target in zip((query_ref, key_ref, value_ref), (begun_query, begun_key, begun_value)):
        target[...] = jnp.dot(normed[...], weight_ref[:channels, :], preferred_element_type=jnp.float32)
    copy.wait()


def main_kernel(
    near_ref, far_ref, other_near_ref, other_far_ref, query_ref, key_ref, value_ref, begun_query, begun_key, begun_value,
    in_out_ref, early_taps, last_tap,
    own_mixed, activated, send_ref,
    normed, queries, keyed, valued, mixed, resid, projected,
):
    frames, rows, cols, channels = resid.shape
    own_frames = own_mixed.shape[0] // cols
    tokens = frames * rows * cols
    frame_tokens = rows * cols
    space = lax.axis_index("space")
    block = lax.axis_index("tm")
    half = lax.axis_index("chan")
    width = D // NGROUP
    count = tokens * width

    blocks = frames // own_frames

    layout = (own_frames, cols, rows, blocks)
    mine, other = core_chunks(near_ref, far_ref, layout), core_chunks(other_near_ref, other_far_ref, layout)
    norm_chunks(other, core_gain(other_near_ref, 0), normed)
    in_channels = early_taps.shape[3]
    mine_in = block == half
    spans = [slice(frame * frame_tokens, (frame + 1) * frame_tokens) for frame in range(frames)]
    for weight_ref, begun_ref, target in ((query_ref, begun_query, queries), (key_ref, begun_key, keyed)):
        term = jnp.dot(normed[...], weight_ref[channels:, :], preferred_element_type=jnp.float32)
        target[...] = (begun_ref[...] + term).astype(jnp.bfloat16)
    scores = [
        lax.dot_general(queries[at, :], keyed[at, :], (((1,), (1,)), ((), ())), preferred_element_type=jnp.float32)
        for at in spans
    ]
    for weight_ref, begun_ref, target in ((value_ref, begun_value, valued),):
        term = jnp.dot(normed[...], weight_ref[channels:, :], preferred_element_type=jnp.float32)
        target[...] = (begun_ref[...] + term).astype(jnp.bfloat16)
    for at, score in zip(spans, scores):
        peak = jnp.max(score, axis=1, keepdims=True)
        weights = jnp.exp2((score - peak) * (D ** (-0.5) * LOG2_E))
        mass = jnp.sum(weights, axis=1, keepdims=True)
        blend = jnp.dot(weights.astype(jnp.bfloat16), valued[at, :], preferred_element_type=jnp.float32)
        mixed[at, :] = (blend * (1.0 / mass)).astype(jnp.bfloat16)
    projected[...] = jnp.dot(mixed[...], in_out_ref[...], preferred_element_type=jnp.float32).astype(jnp.bfloat16)
    totals = None
    for chunk, ((ref, at), (other_ref, _)) in enumerate(zip(mine, other)):
        source = jnp.where(mine_in, ref[at, :], other_ref[at, :]).astype(jnp.float32)
        total = source + projected[chunk * cols : (chunk + 1) * cols, :].astype(jnp.float32)
        resid[chunk // rows, chunk % rows] = total
        totals = add_chunk(totals, total)
    size = own_mixed.shape[0] // own_frames
    for frame, at in enumerate(spans[:own_frames]):
        own_mixed[frame * size : (frame + 1) * size, :] = mixed[at.start : at.start + size, :]

    centre, scale = chunk_statistics(totals, count)
    scale = 0.5 * scale * jnp.where(mine_in, core_gain(near_ref, 1), core_gain(other_near_ref, 1))
    activated[:, 0:2] = jnp.zeros((3, 2, cols, in_channels), jnp.bfloat16)
    for tap in range(3):
        row = space + (tap - 1)
        inside = jnp.logical_and(row >= 0, row < rows)
        place = jnp.where(inside, space ^ row, 0)
        row_scale = jnp.where(inside, scale, 0.0)
        for frame in range(frames):
            relative = ((frame // own_frames) ^ block) * own_frames + frame % own_frames
            halved = (resid[relative, place] - centre) * row_scale
            activated[tap, frame + 2] = (halved + halved * jnp.tanh(halved)).astype(jnp.bfloat16)

    send_ref[...] = partial_conv(activated, early_taps, last_tap, 1 - block, own_frames).astype(jnp.bfloat16)


def partial_conv(activated, early_taps, last_tap, block, frames):
    cols, in_channels = activated.shape[2:]
    tokens = frames * cols
    taps = [ref.at[tap] for ref in (early_taps, last_tap) for tap in range(ref.shape[0])]
    columns = []
    for col_tap in range(3):
        total = None
        for time_tap in range(3):
            start = block * frames + time_tap
            windows = [activated[row_tap, pl.ds(start, frames)].reshape(tokens, in_channels) for row_tap in range(3)]
            term = jnp.dot(
                jnp.concatenate(windows, axis=1),
                taps[time_tap][:, col_tap].reshape(3 * in_channels, -1),
                preferred_element_type=jnp.float32,
            )
            total = term if total is None else total + term
        columns.append(total)
    place = lax.broadcasted_iota(jnp.int32, columns[0].shape, 0) % cols
    left = jnp.where(place == 0, 0.0, pltpu.roll(columns[0], 1, 0))
    right = jnp.where(place == cols - 1, 0.0, pltpu.roll(columns[2], tokens - 1, 0))
    return columns[1] + left + right


def own_kernel(activated, early_taps, last_tap, own_mixed, own_out_ref, attended_hbm, keep_ref, attended_ref, sent):
    attended_ref[...] = jnp.dot(
        own_mixed[...], own_out_ref[...], preferred_element_type=jnp.float32
    ).astype(jnp.bfloat16).reshape(attended_ref.shape)
    copy = pltpu.make_async_copy(attended_ref, attended_hbm, sent)
    copy.start()
    keep_ref[...] = partial_conv(activated, early_taps, last_tap, lax.axis_index("tm"), attended_ref.shape[0])
    copy.wait()


def gathered_plan(
    hidden_states, first_gain, second_gain, query_weight, key_weight, value_weight, out_weight, conv_kernel
):
    frames, _, cols, channels = hidden_states.shape
    rows, blocks = lax.axis_size("space"), lax.axis_size("tm")
    own = hidden_states.reshape(frames * cols, channels)
    gains = (first_gain.reshape(1, channels), second_gain.reshape(1, channels))
    by_row = {row: exchange(own, "space", row) for row in range(rows - 1, 0, -1)}
    first = exchange(own, "tm", 1)
    onward = {row: exchange(piece, "tm", 1) for row, piece in by_row.items() if row >= rows // 2}
    for row in range(1, rows // 2):
        onward[row] = exchange(own, ("space", "tm"), row * blocks + 1)
    staged = (query_weight, key_weight, value_weight, out_weight, own, *gains, conv_kernel)
    *weights, in_out, own_out, own_staged, first_gain, second_gain, early_taps = stage(staged, by_row[rows // 2])
    near = [own_staged, first]
    for row in range(1, rows // 2):
        near += [by_row[row], onward[row]]
    far = [piece for row in range(rows // 2, rows) for piece in (by_row[row], onward[row])]
    near_mine = pack(near_kernel, near, "near", (first_gain, second_gain))
    near_other = exchange(near_mine, "chan", 1)
    far_mine = pack(pack_kernel, far, "far")
    far_other = exchange(far_mine, "chan", 1)
    in_channels, out_channels = conv_kernel.shape[3:]
    tokens = blocks * frames * rows * cols
    in_vmem = pl.BlockSpec(memory_space=pltpu.VMEM)
    *begun, last_tap = pl.pallas_call(
        functools.partial(mine_kernel, layout=(frames, cols, rows, blocks)),
        out_shape=(jax.ShapeDtypeStruct((tokens, D), jnp.float32),) * 3
        + (jax.ShapeDtypeStruct((1, *conv_kernel.shape[1:]), conv_kernel.dtype),),
        in_specs=[in_vmem] * 5 + [pl.BlockSpec(memory_space=pltpu.HBM)],
        out_specs=(in_vmem,) * 4,
        scratch_shapes=[pltpu.VMEM((tokens, channels), jnp.bfloat16), pltpu.SemaphoreType.DMA],
        compiler_params=pltpu.CompilerParams(vmem_limit_bytes=8 * 1024 * 1024),
        name="mine",
    )(near_mine, far_mine, *weights, in_hbm(conv_kernel))
    own_mixed, activated, send = pl.pallas_call(
        main_kernel,
        out_shape=(
            jax.ShapeDtypeStruct((frames * cols, D), jnp.bfloat16),
            jax.ShapeDtypeStruct((3, blocks * frames + 2, cols, in_channels), jnp.bfloat16),
            jax.ShapeDtypeStruct((frames * cols, out_channels), jnp.bfloat16),
        ),
        in_specs=[in_vmem] * 13,
        out_specs=(in_vmem,) * 3,
        scratch_shapes=[pltpu.VMEM((tokens, channels), jnp.bfloat16)]
        + [pltpu.VMEM((tokens, D), jnp.bfloat16)] * 4
        + [pltpu.VMEM((blocks * frames, rows, cols, in_channels), jnp.float32)]
        + [pltpu.VMEM((tokens, in_channels), jnp.bfloat16)],
        compiler_params=pltpu.CompilerParams(vmem_limit_bytes=24 * 1024 * 1024),
        name="block",
    )(near_mine, far_mine, near_other, far_other, *weights, *begun, in_out, early_taps, last_tap)
    received = exchange(send, "tm", 1)
    attended, keep = pl.pallas_call(
        own_kernel,
        out_shape=(
            jax.ShapeDtypeStruct((frames, 1, cols, channels), jnp.bfloat16),
            jax.ShapeDtypeStruct((frames * cols, out_channels), jnp.float32),
        ),
        in_specs=[in_vmem] * 5,
        out_specs=(pl.BlockSpec(memory_space=pl.ANY), in_vmem),
        scratch_shapes=[pltpu.VMEM((frames, 1, cols, channels), jnp.bfloat16), pltpu.SemaphoreType.DMA],
        compiler_params=pltpu.CompilerParams(vmem_limit_bytes=4 * 1024 * 1024),
        name="own",
    )(activated, early_taps, last_tap, own_mixed, own_out)
    total = keep + received.astype(jnp.float32)
    return attended, total.astype(jnp.bfloat16).reshape(frames, 1, cols, out_channels)


def power_of_two(count):
    return count & (count - 1) == 0


def on_device(hidden_states, *others):
    frames, rows, cols, channels = hidden_states.shape
    spaces, blocks = lax.axis_size("space"), lax.axis_size("tm")
    tokens = frames * blocks * spaces * rows * cols
    fits = tokens * D <= 2 ** 20 and rows == 1 and lax.axis_size("chan") == 2 and blocks == 2
    if fits and power_of_two(spaces):
        return gathered_plan(hidden_states, *others)
    return split_plan(hidden_states, *others)


def solution(mesh):
    placed = (
        P(("groups", "tm"), "space", None, "chan"),
        P("chan"),
        P("chan"),
        P(),
        P(),
        P(),
        P(),
        P(None, None, None, "tm", "chan"),
    )
    return jax.shard_map(
        on_device,
        mesh=mesh,
        in_specs=placed,
        out_specs=(
            P(("groups", "tm"), "space", None, "chan"),
            P(("groups", "tm"), "space", None, "chan"),
        ),
        check_vma=False,
    )
```
